256 devices in a mesh: section: 4 (over y), seq: 64 (over x, z, core).
Axes of the slice: x: 4, y: 4, z: 8, core: 2. Of those that a mesh axis runs over, the one named last changes fastest.
Arguments:
- arriving: bfloat16 [4, 32768, 1536], P('section', 'seq'), may hold values from -6 to 6
- queued: bfloat16 [32768, 1536], P('seq'), may hold values from -6 to 6
- sequence_norm_gain: float32 [4, 1536], P('section'), may hold values from 0.1 to 1.9
- block_factor: bfloat16 [4, 128, 256, 256], P('section', 'seq'), may hold values from -0.375 to 0.375
- cross_factor: bfloat16 [4, 256, 128, 128], P('section', 'seq'), may hold values from -0.5 to 0.5
- channel_gain: float32 [4, 1536], P('section'), may hold values from 0.1 to 1.9
- up_weight: bfloat16 [4, 4, 384, 1024], P('section'), may hold values from -0.3125 to 0.3125
- down_weight: bfloat16 [4, 4, 1024, 384], P('section'), may hold values from -0.1875 to 0.1875
Outputs:
- leading_sequence_output: bfloat16 [4, 32768, 1536], P('section', 'seq')
- second_output: bfloat16 [4, 32768, 1536], P('section', 'seq')
The draws below stay inside these ranges and needn't reach their ends.
All inputs are finite; a program needn't handle non-finite values.
Results may differ from the reference program's by a relative error of at most 0.011.
Values may be sent and summed in bfloat16 or wider, within the bound.
No kernel may reach another device: no remote copies, remote signals or barrier semaphores. Data moves between devices by JAX's collectives and lax.ppermute only.
A program may use at most 128 MiB of HBM per device.

```python
import jax
import jax.numpy as jnp
from jax import lax

D = 1536
FF = 4096
CHANNEL_GROUPS = 4
NBLK = 128
BS = 256
SEQ = 32768
N_SECTION = 4


def steps_of(stream_key, extent, pieces, low, high):
    level, own = 1.0, jax.random.fold_in(stream_key, 6)
    for position, shards_of in pieces:
        heights = jnp.exp(jax.random.uniform(jax.random.fold_in(own, position), (shards_of,), jnp.float32, low / len(pieces), high / len(pieces)))
        level = level * jnp.repeat(heights, extent[position] // shards_of).reshape([-1 if axis == position else 1 for axis in range(len(extent))])
    return level


def scatter_about(own_key, dims, spread, most, split=(), held_as=jnp.bfloat16):
    values = spread * jax.random.normal(own_key, dims, jnp.float32)
    if split:
        values = values * steps_of(own_key, dims, split, -0.22, 0.18)
    return jnp.clip(values, -most, most).astype(held_as)


def setup_inputs(seed: int = 0) -> dict:
    arg_keys = jax.random.split(jax.random.key(seed), 9)
    return {
        "arriving": scatter_about(arg_keys[0], (N_SECTION, SEQ, D), 1.0, 6.0, ((0, 4), (1, 64))),
        "queued": scatter_about(arg_keys[1], (SEQ, D), 1.0, 6.0, ((0, 64),)),
        "sequence_norm_gain": jnp.clip(1.0 + 0.18 * jax.random.normal(arg_keys[2], (N_SECTION, D), jnp.float32), 0.1, 1.9),
        "block_factor": scatter_about(arg_keys[3], (N_SECTION, NBLK, BS, BS), BS ** -0.5, 0.375, ((0, 4), (1, 64))),
        "cross_factor": scatter_about(arg_keys[4], (N_SECTION, BS, NBLK, NBLK), NBLK ** -0.5, 0.5, ((0, 4), (1, 64))),
        "channel_gain": jnp.clip(1.0 + 0.18 * jax.random.normal(arg_keys[5], (N_SECTION, D), jnp.float32), 0.1, 1.9),
        "up_weight": scatter_about(arg_keys[6], (N_SECTION, CHANNEL_GROUPS, D // CHANNEL_GROUPS, FF // CHANNEL_GROUPS), (D // CHANNEL_GROUPS) ** -0.5, 0.3125, ((0, 4),)),
        "down_weight": scatter_about(arg_keys[7], (N_SECTION, CHANNEL_GROUPS, FF // CHANNEL_GROUPS, D // CHANNEL_GROUPS), (FF // CHANNEL_GROUPS) ** -0.5, 0.1875, ((0, 4),)),
    }


norm_epsilon_floor = 1e-05

def normalize(values, gain):
    scale = lax.rsqrt(lax.optimization_barrier(jnp.mean(values * values, axis=-1, keepdims=True)) + norm_epsilon_floor)
    return (values * scale * gain).astype(jnp.bfloat16)

def apply_layer(stream, mix_row, block_mats, cross_mats, channel_vector, up_mats, down_matrices):
    stream_wide = stream.astype(jnp.float32)
    normed_in = normalize(stream_wide, mix_row).reshape(NBLK, BS, D)
    within = jnp.einsum('ipk,ikd->ipd', block_mats.astype(jnp.float32), normed_in.astype(jnp.float32)).astype(jnp.bfloat16)
    across = jnp.einsum('jim,mjd->ijd', cross_mats.astype(jnp.float32), within.astype(jnp.float32)).astype(jnp.bfloat16)
    residual = stream_wide + across.reshape(SEQ, D).astype(jnp.float32)
    normed_mid = normalize(residual, channel_vector).reshape(SEQ, CHANNEL_GROUPS, D // CHANNEL_GROUPS)
    expanded = jnp.einsum('tgc,gcf->tgf', normed_mid.astype(jnp.float32), up_mats.astype(jnp.float32))
    gelu_activations = jax.nn.gelu(expanded, approximate=True).astype(jnp.bfloat16)
    reduced_hidden = jnp.einsum('shb,hbl->shl', gelu_activations.astype(jnp.float32), down_matrices.astype(jnp.float32))
    return (residual + reduced_hidden.reshape(SEQ, D)).astype(jnp.bfloat16)

def reference(arriving, queued, sequence_norm_gain, block_factor, cross_factor, channel_gain, up_weight, down_weight):
    firsts = []
    seconds = []
    for section_number in range(N_SECTION):
        first_result = apply_layer(arriving[section_number], sequence_norm_gain[section_number], block_factor[section_number], cross_factor[section_number], channel_gain[section_number], up_weight[section_number], down_weight[section_number])
        if section_number == 0:
            entering = queued
        else:
            entering = firsts[section_number - 1]
        second_result = apply_layer(entering, sequence_norm_gain[section_number], block_factor[section_number], cross_factor[section_number], channel_gain[section_number], up_weight[section_number], down_weight[section_number])
        firsts.append(first_result)
        seconds.append(second_result)
    return (jnp.stack(firsts), jnp.stack(seconds))
```

```python
import functools

import jax
import jax.numpy as jnp
from jax import lax
from jax.experimental import pallas as pl
from jax.experimental.pallas import tpu as pltpu
from jax.sharding import PartitionSpec as P

EPS = 1e-05
D = 1536
HALF = D // 2
BLK = 256
DEV = 64
GROUPS = 4
BF = jnp.bfloat16
F32 = jnp.float32


def call(kernel, out_shape, flops, bytes_accessed, transcendentals=0):
    return pl.pallas_call(
        kernel,
        out_shape=out_shape,
        cost_estimate=pl.CostEstimate(
            flops=flops, bytes_accessed=bytes_accessed, transcendentals=transcendentals
        ),
        compiler_params=pltpu.CompilerParams(vmem_limit_bytes=40 * 1024 * 1024),
    )


def dot(a, b):
    return jnp.dot(a, b, preferred_element_type=F32)


def normalize(values, gain):
    scale = lax.rsqrt(jnp.mean(values * values, axis=-1, keepdims=True) + EPS)
    return (values * scale * gain).astype(BF)


def packer(h):
    row = lax.broadcasted_iota(jnp.int32, (2 * BLK, BLK), 0)
    col = lax.broadcasted_iota(jnp.int32, (2 * BLK, BLK), 1)
    hit = ((row // 8) * 4 + row % 4 == col) & ((row % 8) // 4 == h)
    return jnp.where(hit, 1.0, 0.0).astype(BF)


def unpacker(h):
    row = lax.broadcasted_iota(jnp.int32, (BLK, 2 * BLK), 0)
    col = lax.broadcasted_iota(jnp.int32, (BLK, 2 * BLK), 1)
    hit = ((col // 8) * 4 + col % 4 == row) & ((col % 8) // 4 == h)
    return jnp.where(hit, 1.0, 0.0).astype(BF)


def within_of(x, gain, factor):
    normed = normalize(x, gain)
    mixed = dot(factor, normed).astype(BF)
    packed = dot(packer(0), mixed[:, :HALF]) + dot(packer(1), mixed[:, HALF:])
    return packed.astype(BF).reshape(DEV, 8, HALF)


def first_kernel(x_ref, gain_ref, factor_ref, out_ref):
    for b in range(2):
        x = x_ref[b * BLK : (b + 1) * BLK, :].astype(F32)
        out_ref[:, b] = within_of(x, gain_ref[...], factor_ref[b])


def later_kernel(b, flag_ref, x_ref, queued_ref, gain_ref, factor_ref, out_ref, entering_ref):
    x = jnp.where(flag_ref[0] == 0, queued_ref[b * BLK : (b + 1) * BLK, :], x_ref[...])
    entering_ref[...] = x
    out_ref[...] = within_of(x.astype(F32), gain_ref[...], factor_ref[b])


def spread_kernel(cross_ref, out_ref):
    n = 2 * BLK
    row = lax.broadcasted_iota(jnp.int32, (n, n), 0)
    col = lax.broadcasted_iota(jnp.int32, (n, n), 1)
    same = row % 8 == col % 8
    cross = cross_ref[...].reshape(n, 128)
    crow = lax.broadcasted_iota(jnp.int32, (128, n), 0)
    ccol = lax.broadcasted_iota(jnp.int32, (128, n), 1)
    for to in range(2):
        pick = col == (row % 4) * 128 + (row // 8) * 2 + to
        rows = dot(jnp.where(pick, 1.0, 0.0).astype(BF), cross).astype(BF)
        for b in range(2):
            pick = crow == (ccol // 8) * 2 + b
            full = dot(rows, jnp.where(pick, 1.0, 0.0).astype(BF))
            out_ref[to, b] = jnp.where(same, full, 0.0).astype(BF)


def cross_joint_kernel(to, spread_ref, r_ref, out_ref):
    total = dot(spread_ref[to, 0], r_ref[:, 0].reshape(2 * BLK, HALF))
    total += dot(spread_ref[to, 1], r_ref[:, 1].reshape(2 * BLK, HALF))
    out_ref[...] = total.astype(BF).reshape(DEV, 8, HALF)


def cross_both_kernel(spread_ref, r0_ref, r1_ref, out_ref):
    for to in range(2):
        total = dot(spread_ref[to, 0], r0_ref[...].reshape(2 * BLK, HALF))
        total += dot(spread_ref[to, 1], r1_ref[...].reshape(2 * BLK, HALF))
        out_ref[:, to] = total.astype(BF).reshape(DEV, 8, HALF)


def channel_rows(x, packed, gain, up_ref, down_ref, store):
    packed = packed.reshape(2 * BLK, HALF)
    across = jnp.concatenate([dot(unpacker(0), packed), dot(unpacker(1), packed)], axis=1)
    residual = x.astype(F32) + across
    normed = normalize(residual, gain)
    width = D // GROUPS
    for g in range(GROUPS):
        part = slice(g * width, (g + 1) * width)
        hidden = dot(normed[:, part], up_ref[g])
        act = jax.nn.gelu(hidden, approximate=True).astype(BF)
        store(part, (residual[:, part] + dot(act, down_ref[g])).astype(BF))


def channel_kernel(b, x_ref, packed_ref, gain_ref, up_ref, down_ref, out_ref):
    def store(part, value):
        out_ref[:, part] = value

    x = x_ref[b * BLK : (b + 1) * BLK, :]
    channel_rows(x, packed_ref[...], gain_ref[...], up_ref, down_ref, store)


def channel_both_kernel(x0_ref, x1_ref, packed_ref, gain_ref, up_ref, down_ref, out_ref):
    for b, x_ref in enumerate((x0_ref, x1_ref)):

        def store(part, value):
            out_ref[b * BLK : (b + 1) * BLK, part] = value

        channel_rows(x_ref[...], packed_ref[:, b], gain_ref[...], up_ref, down_ref, store)


def shape(*dims):
    return jax.ShapeDtypeStruct(dims, BF)


def exchange(value):
    return lax.all_to_all(value, "seq", split_axis=0, concat_axis=0, tiled=True)


def per_device(arriving, queued, norm_gain, block_factor, cross_factor, channel_gain, up, down):
    section = lax.axis_index("section")
    flag = jnp.full((1,), section, jnp.int32)
    x = arriving[0]
    factor, cross, up, down = block_factor[0], cross_factor[0], up[0], down[0]
    count = lax.axis_size("section")
    ahead = [(s, s + 1) for s in range(count - 1)]

    sent = call(first_kernel, shape(DEV, 2, 8, HALF), 1_200_000_000, 4_000_000)(
        x, norm_gain, factor
    )
    columns = exchange(sent)
    spread = call(spread_kernel, shape(2, 2, 2 * BLK, 2 * BLK), 500_000_000, 2_300_000)(cross)

    back = []
    for to in range(2):
        out = call(
            functools.partial(cross_joint_kernel, to), shape(DEV, 8, HALF), 800_000_000, 4_000_000
        )(spread, columns)
        back.append(exchange(out))

    firsts, entering, columns = [], [], []
    for b in range(2):
        first = call(
            functools.partial(channel_kernel, b), shape(BLK, D), 2_000_000_000, 9_000_000, 1_000_000
        )(x, back[b], channel_gain, up, down)
        firsts.append(first)
        received = lax.ppermute(first, "section", ahead)
        specs = [pl.BlockSpec(memory_space=pltpu.SMEM)] + [
            pl.BlockSpec(memory_space=pltpu.VMEM)
        ] * 4
        sent, enters = pl.pallas_call(
            functools.partial(later_kernel, b),
            out_shape=(shape(DEV, 8, HALF), shape(BLK, D)),
            in_specs=specs,
            cost_estimate=pl.CostEstimate(
                flops=600_000_000, bytes_accessed=4_000_000, transcendentals=0
            ),
            compiler_params=pltpu.CompilerParams(vmem_limit_bytes=40 * 1024 * 1024),
        )(flag, received, queued, norm_gain, factor)
        entering.append(enters)
        columns.append(exchange(sent))

    out = call(cross_both_kernel, shape(DEV, 2, 8, HALF), 1_600_000_000, 5_000_000)(
        spread, columns[0], columns[1]
    )
    packed = exchange(out)
    second = call(channel_both_kernel, shape(2 * BLK, D), 4_000_000_000, 11_000_000, 2_000_000)(
        entering[0], entering[1], packed, channel_gain, up, down
    )
    return jnp.concatenate(firsts, axis=0)[None], second[None]


def solution(mesh):
    placed = (
        P("section", "seq", None),
        P("seq", None),
        P("section", None),
        P("section", "seq", None, None),
        P("section", "seq", None, None),
        P("section", None),
        P("section", None, None, None),
        P("section", None, None, None),
    )
    return jax.shard_map(
        per_device,
        mesh=mesh,
        in_specs=placed,
        out_specs=(P("section", "seq", None), P("section", "seq", None)),
        check_vma=False,
    )
```

```python
import functools

import jax
import jax.numpy as jnp
from jax import lax
from jax.experimental import pallas as pl
from jax.experimental.pallas import tpu as pltpu
from jax.sharding import PartitionSpec as P

EPS = 1e-05
D = 1536
HALF = D // 2
BLK = 256
DEV = 64
GROUPS = 4
BF = jnp.bfloat16
F32 = jnp.float32


def call(kernel, out_shape, flops, bytes_accessed, transcendentals=0, scalars=0, arrays=0):
    specs = None
    if scalars:
        specs = [pl.BlockSpec(memory_space=pltpu.SMEM)] * scalars
        specs += [pl.BlockSpec(memory_space=pltpu.VMEM)] * arrays
    return pl.pallas_call(
        kernel,
        out_shape=out_shape,
        **({"in_specs": specs} if specs else {}),
        cost_estimate=pl.CostEstimate(
            flops=flops, bytes_accessed=bytes_accessed, transcendentals=transcendentals
        ),
        compiler_params=pltpu.CompilerParams(vmem_limit_bytes=44 * 1024 * 1024),
    )


def dot(a, b):
    return jnp.dot(a, b, preferred_element_type=F32)


def onehot(rows, cols, hit):
    r = lax.broadcasted_iota(jnp.int32, (rows, cols), 0)
    c = lax.broadcasted_iota(jnp.int32, (rows, cols), 1)
    return jnp.where(hit(r, c), 1.0, 0.0).astype(BF)


def packed_at(r, j, c, h, b):
    return (((r >> 3) * 4 + 2 * c + (r & 1)) == j) & (((r >> 1) & 3) == 2 * h + b)


def pack(c, h, b):
    return onehot(2 * BLK, BLK, lambda r, j: packed_at(r, j, c, h, b))


def unpack(c, h, b):
    return onehot(BLK, 2 * BLK, lambda j, r: packed_at(r, j, c, h, b))


def unpack_compact(h):
    return onehot(
        BLK, 2 * BLK, lambda q, r: r == ((q & 127) >> 1) * 8 + 4 * h + 2 * (q >> 7) + (q & 1)
    )


def pick(c):
    return onehot(BLK // 2, BLK, lambda q, j: j == (q >> 1) * 4 + 2 * c + (q & 1))


def place(c):
    return onehot(BLK, BLK // 2, lambda j, q: j == (q >> 1) * 4 + 2 * c + (q & 1))


def normalize(values, gain):
    scale = lax.rsqrt(jnp.mean(values * values, axis=-1, keepdims=True) + EPS)
    return (values * scale * gain).astype(BF)


def packed_part(c, mixed):
    total = None
    for b in range(2):
        for h in range(2):
            term = dot(pack(c, h, b), mixed[b][:, h * HALF : (h + 1) * HALF])
            total = term if total is None else total + term
    return total.astype(BF).reshape(DEV, 8, HALF)


def first_kernel(x_ref, gain_ref, factor_ref, out_ref):
    mixed = []
    for b in range(2):
        x = x_ref[b * BLK : (b + 1) * BLK, :].astype(F32)
        mixed.append(dot(factor_ref[b], normalize(x, gain_ref[...])).astype(BF))
    for c in range(2):
        out_ref[:, c] = packed_part(c, mixed)


def spread_kernel(cross_ref, out_ref):
    n = 2 * BLK
    row = lax.broadcasted_iota(jnp.int32, (n, n), 0)
    col = lax.broadcasted_iota(jnp.int32, (n, n), 1)
    same = ((row ^ col) & 5) == 0
    cross = cross_ref[...].reshape(n, 128)
    columns = onehot(128, n, lambda m, k: m == (k >> 3) * 2 + ((k >> 1) & 1))
    for c in range(2):
        rows = onehot(
            n, n, lambda r, k: k == (2 * c + (r & 1)) * 128 + (r >> 3) * 2 + ((r >> 1) & 1)
        )
        full = dot(dot(rows, cross).astype(BF), columns)
        out_ref[c] = jnp.where(same, full, 0.0).astype(BF)


def cross_both_kernel(spread_ref, r_ref, out_ref):
    for c in range(2):
        total = dot(spread_ref[c], r_ref[:, c].reshape(2 * BLK, HALF))
        out_ref[:, c] = total.astype(BF).reshape(DEV, 8, HALF)


def cross_kernel(c, spread_ref, r_ref, out_ref):
    total = dot(spread_ref[c], r_ref[...].reshape(2 * BLK, HALF))
    out_ref[...] = total.astype(BF).reshape(DEV, 8, HALF)


def channel_rows(residual, gain, up_ref, down_ref, store):
    normed = normalize(residual, gain)
    width = D // GROUPS
    for g in range(GROUPS):
        part = slice(g * width, (g + 1) * width)
        hidden = dot(normed[:, part], up_ref[g])
        act = jax.nn.gelu(hidden, approximate=True).astype(BF)
        store(part, (residual[:, part] + dot(act, down_ref[g])).astype(BF))


def middle_kernel(
    flag_ref,
    x_ref,
    across_ref,
    channel_ref,
    up_ref,
    down_ref,
    queued_ref,
    gain_ref,
    factor_ref,
    first_ref,
    kept_ref,
    mixed_ref,
    out_ref,
):
    packed = [across_ref[:, c].reshape(2 * BLK, HALF) for c in range(2)]
    mixed = []
    for b in range(2):
        rows = slice(b * BLK, (b + 1) * BLK)
        across = jnp.concatenate(
            [dot(unpack(0, h, b), packed[0]) + dot(unpack(1, h, b), packed[1]) for h in range(2)],
            axis=1,
        )

        def store(part, value):
            first_ref[rows, part] = value

        residual = x_ref[rows, :].astype(F32) + across
        channel_rows(residual, channel_ref[...], up_ref, down_ref, store)
        first = first_ref[rows, :]
        kept_ref[b * (BLK // 2) : (b + 1) * (BLK // 2), :] = dot(pick(0), first).astype(BF)
        entering = jnp.where(flag_ref[1] == 1, queued_ref[rows, :], first)
        normed = normalize(entering.astype(F32), gain_ref[...])
        mixed.append(dot(factor_ref[b], normed).astype(BF))
        mixed_ref[rows, :] = mixed[b]
    out_ref[...] = packed_part(0, mixed)


def remainder_kernel(first_ref, mixed_ref, kept_ref, out_ref):
    mixed = [mixed_ref[b * BLK : (b + 1) * BLK, :] for b in range(2)]
    out_ref[...] = packed_part(1, mixed)
    for b in range(2):
        first = first_ref[b * BLK : (b + 1) * BLK, :]
        kept_ref[b * (BLK // 2) : (b + 1) * (BLK // 2), :] = dot(pick(1), first).astype(BF)


def last_rows(c, flag_ref, queued_ref, x_ref, across_ref, channel_ref, up_ref, down_ref, store):
    queued = [
        dot(pick(c), queued_ref[b * BLK : (b + 1) * BLK, :]).astype(BF) for b in range(2)
    ]
    x = jnp.where(flag_ref[0] == 1, jnp.concatenate(queued, axis=0), x_ref[...])
    packed = across_ref[...].reshape(2 * BLK, HALF)
    across = jnp.concatenate([dot(unpack_compact(h), packed) for h in range(2)], axis=1)
    channel_rows(x.astype(F32) + across, channel_ref[...], up_ref, down_ref, store)


def last_kernel(
    flag_ref, queued_ref, x_ref, across_ref, channel_ref, up_ref, down_ref, out_ref
):
    def store(part, value):
        out_ref[:, part] = value

    last_rows(
        0, flag_ref, queued_ref, x_ref, across_ref, channel_ref, up_ref, down_ref, store
    )


def final_kernel(
    flag_ref, queued_ref, x_ref, across_ref, channel_ref, up_ref, down_ref, other_ref, out_ref
):
    def store(part, value):
        for b in range(2):
            rows = slice(b * (BLK // 2), (b + 1) * (BLK // 2))
            joined = dot(place(0), other_ref[rows, part]) + dot(place(1), value[rows])
            out_ref[b * BLK : (b + 1) * BLK, part] = joined.astype(BF)

    last_rows(
        1, flag_ref, queued_ref, x_ref, across_ref, channel_ref, up_ref, down_ref, store
    )


def shape(*dims):
    return jax.ShapeDtypeStruct(dims, BF)


def exchange(value):
    return lax.all_to_all(value, "seq", split_axis=0, concat_axis=0, tiled=True)


def per_device(arriving, queued, norm_gain, block_factor, cross_factor, channel_gain, up, down):
    section = lax.axis_index("section")
    count = lax.axis_size("section")
    flags = jnp.stack([section == 0, section == count - 1]).astype(jnp.int32)
    x = arriving[0]
    factor, cross, up, down = block_factor[0], cross_factor[0], up[0], down[0]

    def ahead(value):
        return lax.ppermute(value, "section", [(s, (s + 1) % count) for s in range(count)])

    def behind(value):
        return lax.ppermute(value, "section", [((s + 1) % count, s) for s in range(count)])

    message = shape(DEV, 8, HALF)
    both = shape(DEV, 2, 8, HALF)
    sent = call(first_kernel, both, 2_000_000_000, 4_000_000)(x, norm_gain, factor)
    columns = exchange(sent)
    spread = call(spread_kernel, shape(2, 2 * BLK, 2 * BLK), 400_000_000, 1_300_000)(cross)
    next_gain, next_factor = behind(norm_gain), behind(factor)

    out = call(cross_both_kernel, both, 800_000_000, 4_000_000)(spread, columns)
    across = exchange(out)

    first, kept0, mixed, sent0 = call(
        middle_kernel,
        (shape(2 * BLK, D), shape(BLK, D), shape(2 * BLK, D), message),
        7_000_000_000,
        18_000_000,
        2_000_000,
        1,
        8,
    )(flags, x, across, channel_gain, up, down, queued, next_gain, next_factor)
    columns0 = exchange(sent0)
    kept1, sent1 = call(
        remainder_kernel, (shape(BLK, D), message), 1_000_000_000, 5_000_000
    )(first, mixed)
    x0 = ahead(kept0)
    columns1 = exchange(sent1)
    columns0 = ahead(columns0)
    out0 = call(functools.partial(cross_kernel, 0), message, 400_000_000, 2_000_000)(
        spread, columns0
    )
    across0 = exchange(out0)
    columns1 = ahead(columns1)
    out1 = call(functools.partial(cross_kernel, 1), message, 400_000_000, 2_000_000)(
        spread, columns1
    )
    kept1, out1 = lax.optimization_barrier((kept1, out1))
    x1 = ahead(kept1)
    across1 = exchange(out1)
    other = call(last_kernel, shape(BLK, D), 2_500_000_000, 10_000_000, 1_000_000, 1, 6)(
        flags, queued, x0, across0, channel_gain, up, down
    )
    second = call(final_kernel, shape(2 * BLK, D), 3_000_000_000, 11_000_000, 1_000_000, 1, 7)(
        flags, queued, x1, across1, channel_gain, up, down, other
    )
    return first[None], second[None]


def solution(mesh):
    placed = (
        P("section", "seq", None),
        P("seq", None),
        P("section", None),
        P("section", "seq", None, None),
        P("section", "seq", None, None),
        P("section", None),
        P("section", None, None, None),
        P("section", None, None, None),
    )
    return jax.shard_map(
        per_device,
        mesh=mesh,
        in_specs=placed,
        out_specs=(P("section", "seq", None), P("section", "seq", None)),
        check_vma=False,
    )
```

```python
import functools

import jax
import jax.numpy as jnp
from jax import lax
from jax.experimental import pallas as pl
from jax.experimental.pallas import tpu as pltpu
from jax.sharding import PartitionSpec as P

EPS = 1e-05
D = 1536
HALF = D // 2
BLK = 256
DEV = 64
GROUPS = 4
BF = jnp.bfloat16
F32 = jnp.float32


def call(kernel, out_shape, places, results, cost, scratch=()):
    kinds = {"s": pltpu.SMEM, "v": pltpu.VMEM, "h": pltpu.HBM}
    outs = [pl.BlockSpec(memory_space=kinds[p]) for p in results]
    flops, bytes_accessed, transcendentals = cost
    return pl.pallas_call(
        kernel,
        out_shape=out_shape,
        in_specs=[pl.BlockSpec(memory_space=kinds[p]) for p in places],
        out_specs=outs if len(outs) > 1 else outs[0],
        scratch_shapes=scratch,
        cost_estimate=pl.CostEstimate(
            flops=flops, bytes_accessed=bytes_accessed, transcendentals=transcendentals
        ),
        compiler_params=pltpu.CompilerParams(vmem_limit_bytes=44 * 1024 * 1024),
    )


def copies(pairs, sems):
    started = [
        pltpu.make_async_copy(source, target, sems.at[i])
        for i, (source, target) in enumerate(pairs)
    ]
    for copy in started:
        copy.start()
    return started


def dot(a, b):
    return jnp.dot(a, b, preferred_element_type=F32)


def onehot(rows, cols, hit):
    r = lax.broadcasted_iota(jnp.int32, (rows, cols), 0)
    c = lax.broadcasted_iota(jnp.int32, (rows, cols), 1)
    return jnp.where(hit(r, c), 1.0, 0.0).astype(BF)


def packed_at(r, j, c, h, b):
    return (((r >> 3) * 4 + 2 * c + (r & 1)) == j) & (((r >> 1) & 3) == 2 * h + b)


def pack(c, h, b):
    return onehot(2 * BLK, BLK, lambda r, j: packed_at(r, j, c, h, b))


def unpack(c, h, b):
    return onehot(BLK, 2 * BLK, lambda j, r: packed_at(r, j, c, h, b))


def unpack_compact(h):
    return onehot(
        BLK, 2 * BLK, lambda q, r: r == ((q & 127) >> 1) * 8 + 4 * h + 2 * (q >> 7) + (q & 1)
    )


def pick(c):
    return onehot(BLK // 2, BLK, lambda q, j: j == (q >> 1) * 4 + 2 * c + (q & 1))


def place(c):
    return onehot(BLK, BLK // 2, lambda j, q: j == (q >> 1) * 4 + 2 * c + (q & 1))


def normalize(values, gain):
    scale = lax.rsqrt(jnp.mean(values * values, axis=-1, keepdims=True) + EPS)
    return (values * scale * gain).astype(BF)


def packed_part(packs, mixed):
    total = None
    for b in range(2):
        for h in range(2):
            term = dot(packs(h, b), mixed[b][:, h * HALF : (h + 1) * HALF])
            total = term if total is None else total + term
    return total.astype(BF).reshape(DEV, 8, HALF)


def first_kernel(x_ref, gain_ref, factor_ref, out_ref, x_buf, factor_buf, out_buf, sems, out_sems):
    rows = [pl.ds(b * BLK, BLK) for b in range(2)]
    loads = copies(
        [
            (x_ref.at[rows[0]], x_buf.at[rows[0]]),
            (factor_ref, factor_buf),
            (x_ref.at[rows[1]], x_buf.at[rows[1]]),
        ],
        sems,
    )
    mixed = []
    for b in range(2):
        loads[2 * b].wait()
        normed = normalize(x_buf[rows[b], :].astype(F32), gain_ref[...])
        if b == 0:
            loads[1].wait()
        mixed.append(dot(factor_buf[b], normed).astype(BF))
    stores = []
    for c in range(2):
        out_buf[c] = packed_part(functools.partial(pack, c), mixed)
        stores.append(pltpu.make_async_copy(out_buf.at[c], out_ref.at[:, c], out_sems.at[c]))
        stores[c].start()
    for store in stores:
        store.wait()


def spread_kernel(cross_ref, out_ref, pack_ref, unpack_ref, compact_ref, pick_ref, place_ref):
    n = 2 * BLK
    row = lax.broadcasted_iota(jnp.int32, (n, n), 0)
    col = lax.broadcasted_iota(jnp.int32, (n, n), 1)
    same = ((row ^ col) & 5) == 0
    cross = cross_ref[...].reshape(n, 128)
    columns = onehot(128, n, lambda m, k: m == (k >> 3) * 2 + ((k >> 1) & 1))
    for c in range(2):
        rows = onehot(
            n, n, lambda r, k: k == (2 * c + (r & 1)) * 128 + (r >> 3) * 2 + ((r >> 1) & 1)
        )
        full = dot(dot(rows, cross).astype(BF), columns)
        out_ref[c] = jnp.where(same, full, 0.0).astype(BF)
        for h in range(2):
            for b in range(2):
                pack_ref[c, h, b] = pack(c, h, b)
                unpack_ref[c, h, b] = unpack(c, h, b)
        compact_ref[c] = unpack_compact(c)
        pick_ref[c] = pick(c)
        place_ref[c] = place(c)


def cross_both_kernel(spread_ref, r_ref, out_ref):
    for c in range(2):
        total = dot(spread_ref[c], r_ref[:, c].reshape(2 * BLK, HALF))
        out_ref[:, c] = total.astype(BF).reshape(DEV, 8, HALF)


def cross_kernel(c, spread_ref, r_ref, out_ref):
    total = dot(spread_ref[c], r_ref[...].reshape(2 * BLK, HALF))
    out_ref[...] = total.astype(BF).reshape(DEV, 8, HALF)


def gelu(hidden):
    value = hidden.astype(BF)
    half = value * BF(0.5)
    inner = value * (BF(0.7978845608028654) + BF(0.7978845608028654 * 0.044715) * (value * value))
    return half + half * jnp.tanh(inner)


def channel_rows(residual, gain, up, down, store):
    normed = normalize(residual, gain)
    width = D // GROUPS
    for g in range(GROUPS):
        part = slice(g * width, (g + 1) * width)
        act = gelu(dot(normed[:, part], up(g)))
        store(g, part, (residual[:, part] + dot(act, down(g))).astype(BF))


def weight_loads(up_ref, down_ref, up_buf, down_buf, sems):
    pairs = []
    for g in range(GROUPS):
        pairs += [(up_ref.at[g], up_buf.at[g]), (down_ref.at[g], down_buf.at[g])]
    loads = copies(pairs, sems)
    waited = set()

    def get(k, buf, g):
        if (k, g) not in waited:
            waited.add((k, g))
            loads[2 * g + k].wait()
        return buf[g]

    return functools.partial(get, 0, up_buf), functools.partial(get, 1, down_buf)


def middle_kernel(
    flag_ref,
    x_ref,
    across_ref,
    channel_ref,
    up_ref,
    down_ref,
    queued_ref,
    gain_ref,
    factor_ref,
    pack_ref,
    unpack_ref,
    pick_ref,
    first_ref,
    kept_ref,
    mixed_ref,
    out_ref,
    across_buf,
    up_buf,
    down_buf,
    first_buf,
    out_buf,
    sems,
    weight_sems,
):
    loads = copies(
        [(across_ref.at[:, 0], across_buf.at[0]), (across_ref.at[:, 1], across_buf.at[1])],
        sems,
    )
    up, down = weight_loads(up_ref, down_ref, up_buf, down_buf, weight_sems)
    for load in loads:
        load.wait()
    packed = [across_buf[c].reshape(2 * BLK, HALF) for c in range(2)]
    mixed, stores = [], []
    for b in range(2):
        rows = slice(b * BLK, (b + 1) * BLK)
        across = jnp.concatenate(
            [
                dot(unpack_ref[0, h, b], packed[0]) + dot(unpack_ref[1, h, b], packed[1])
                for h in range(2)
            ],
            axis=1,
        )

        def store(g, part, value):
            first_buf[rows, part] = value

        residual = x_ref[rows, :].astype(F32) + across
        channel_rows(residual, channel_ref[...], up, down, store)
        window = pl.ds(b * BLK, BLK)
        stores.append(
            pltpu.make_async_copy(first_buf.at[window], first_ref.at[window], sems.at[2 + b])
        )
        stores[b].start()
        first = first_buf[rows, :]
        kept_ref[b * (BLK // 2) : (b + 1) * (BLK // 2), :] = dot(pick_ref[0], first).astype(BF)
        entering = jnp.where(flag_ref[1] == 1, queued_ref[rows, :], first)
        normed = normalize(entering.astype(F32), gain_ref[...])
        mixed.append(dot(factor_ref[b], normed).astype(BF))
        mixed_ref[rows, :] = mixed[b]
    out_buf[...] = packed_part(lambda h, b: pack_ref[0, h, b], mixed)
    stores.append(pltpu.make_async_copy(out_buf, out_ref, sems.at[4]))
    stores[2].start()
    for store in stores:
        store.wait()


def remainder_kernel(first_ref, mixed_ref, pack_ref, pick_ref, kept_ref, out_ref):
    mixed = [mixed_ref[b * BLK : (b + 1) * BLK, :] for b in range(2)]
    out_ref[...] = packed_part(lambda h, b: pack_ref[1, h, b], mixed)
    for b in range(2):
        first = first_ref[b * BLK : (b + 1) * BLK, :]
        kept_ref[b * (BLK // 2) : (b + 1) * (BLK // 2), :] = dot(pick_ref[1], first).astype(BF)


def last_rows(c, flag_ref, queued_ref, x_ref, pick_ref, compact_ref, across_buf, load):
    queued = [
        dot(pick_ref[c], queued_ref[b * BLK : (b + 1) * BLK, :]).astype(BF) for b in range(2)
    ]
    x = jnp.where(flag_ref[0] == 1, jnp.concatenate(queued, axis=0), x_ref[...])
    load.wait()
    packed = across_buf[...].reshape(2 * BLK, HALF)
    across = jnp.concatenate([dot(compact_ref[h], packed) for h in range(2)], axis=1)
    return x.astype(F32) + across


def last_kernel(
    flag_ref,
    queued_ref,
    x_ref,
    across_ref,
    channel_ref,
    up_ref,
    down_ref,
    pick_ref,
    compact_ref,
    out_ref,
    across_buf,
    up_buf,
    down_buf,
    sems,
    weight_sems,
):
    (load,) = copies([(across_ref, across_buf)], sems)
    up, down = weight_loads(up_ref, down_ref, up_buf, down_buf, weight_sems)

    def store(g, part, value):
        out_ref[:, part] = value

    residual = last_rows(
        0, flag_ref, queued_ref, x_ref, pick_ref, compact_ref, across_buf, load
    )
    channel_rows(residual, channel_ref[...], up, down, store)


def final_kernel(
    flag_ref,
    queued_ref,
    x_ref,
    across_ref,
    channel_ref,
    up_ref,
    down_ref,
    pick_ref,
    compact_ref,
    place_ref,
    other_ref,
    out_ref,
    across_buf,
    up_buf,
    down_buf,
    out_buf,
    sems,
    weight_sems,
    out_sems,
):
    (load,) = copies([(across_ref, across_buf)], sems)
    up, down = weight_loads(up_ref, down_ref, up_buf, down_buf, weight_sems)
    stores = []

    def store(g, part, value):
        for b in range(2):
            rows = slice(b * (BLK // 2), (b + 1) * (BLK // 2))
            joined = dot(place_ref[0], other_ref[rows, part]) + dot(place_ref[1], value[rows])
            out_buf[b * BLK : (b + 1) * BLK, part] = joined.astype(BF)
        width = pl.ds(part.start, part.stop - part.start)
        stores.append(
            pltpu.make_async_copy(out_buf.at[:, width], out_ref.at[:, width], out_sems.at[g])
        )
        stores[g].start()

    residual = last_rows(
        1, flag_ref, queued_ref, x_ref, pick_ref, compact_ref, across_buf, load
    )
    channel_rows(residual, channel_ref[...], up, down, store)
    for copy in stores:
        copy.wait()


def shape(*dims):
    return jax.ShapeDtypeStruct(dims, BF)


def hbm(value):
    return pltpu.with_memory_space_constraint(value, pltpu.HBM)


def exchange(value):
    return lax.all_to_all(value, "seq", split_axis=0, concat_axis=0, tiled=True)


def per_device(arriving, queued, norm_gain, block_factor, cross_factor, channel_gain, up, down):
    section = lax.axis_index("section")
    count = lax.axis_size("section")
    flags = jnp.stack([section == 0, section == count - 1]).astype(jnp.int32)
    x = arriving[0]
    factor, cross = block_factor[0], cross_factor[0]
    up, down, held_x, held_factor = (hbm(v) for v in (up[0], down[0], x, factor))

    def ahead(value):
        return lax.ppermute(value, "section", [(s, (s + 1) % count) for s in range(count)])

    def behind(value):
        return lax.ppermute(value, "section", [((s + 1) % count, s) for s in range(count)])

    message = shape(DEV, 8, HALF)
    both = shape(DEV, 2, 8, HALF)
    sequence, part_rows = shape(2 * BLK, D), shape(BLK, D)
    message_buf = pltpu.VMEM((DEV, 8, HALF), BF)
    pair_buf = pltpu.VMEM((2, DEV, 8, HALF), BF)
    sequence_buf = pltpu.VMEM((2 * BLK, D), BF)
    weight_bufs = [pltpu.VMEM(up.shape, BF), pltpu.VMEM(down.shape, BF)]
    weight_sems = pltpu.SemaphoreType.DMA((2 * GROUPS,))

    def sems(n):
        return pltpu.SemaphoreType.DMA((n,))

    sent = call(
        first_kernel,
        both,
        "hvh",
        "h",
        (2_000_000_000, 4_000_000, 0),
        [sequence_buf, pltpu.VMEM(factor.shape, BF), pair_buf, sems(3), sems(2)],
    )(held_x, norm_gain, held_factor)
    columns = exchange(sent)
    spread, packs, unpacks, compact, picks, places = call(
        spread_kernel,
        (
            shape(2, 2 * BLK, 2 * BLK),
            shape(2, 2, 2, 2 * BLK, BLK),
            shape(2, 2, 2, BLK, 2 * BLK),
            shape(2, BLK, 2 * BLK),
            shape(2, BLK // 2, BLK),
            shape(2, BLK, BLK // 2),
        ),
        "v",
        "vvvvvv",
        (400_000_000, 6_000_000, 0),
    )(cross)
    next_gain, next_factor = behind(norm_gain), behind(factor)

    out = call(cross_both_kernel, both, "vv", "v", (800_000_000, 4_000_000, 0))(spread, columns)
    across = hbm(exchange(out))

    first, kept0, mixed, sent0 = call(
        middle_kernel,
        (sequence, part_rows, sequence, message),
        "svhvhhvvvvvv",
        "hvvh",
        (7_000_000_000, 18_000_000, 2_000_000),
        [pair_buf, *weight_bufs, sequence_buf, message_buf, sems(5), weight_sems],
    )(
        flags,
        x,
        across,
        channel_gain,
        up,
        down,
        queued,
        next_gain,
        next_factor,
        packs,
        unpacks,
        picks,
    )
    x0 = ahead(kept0)
    columns0 = exchange(sent0)
    columns0, x0 = lax.optimization_barrier((columns0, x0))
    kept1, sent1 = call(
        remainder_kernel, (part_rows, message), "vvvv", "vv", (1_000_000_000, 5_000_000, 0)
    )(first, mixed, packs, picks)
    columns0, sent1 = lax.optimization_barrier((columns0, sent1))
    columns0 = ahead(columns0)
    columns1 = exchange(sent1)
    out0 = call(
        functools.partial(cross_kernel, 0), message, "vv", "v", (400_000_000, 2_000_000, 0)
    )(spread, columns0)
    across0 = hbm(exchange(out0))
    columns1 = ahead(columns1)
    kept1, columns1 = lax.optimization_barrier((kept1, columns1))
    x1 = ahead(kept1)
    out1 = call(
        functools.partial(cross_kernel, 1), message, "vv", "v", (400_000_000, 2_000_000, 0)
    )(spread, columns1)
    across1 = hbm(exchange(out1))
    other = call(
        last_kernel,
        part_rows,
        "svvhvhhvv",
        "v",
        (2_500_000_000, 10_000_000, 1_000_000),
        [message_buf, *weight_bufs, sems(1), weight_sems],
    )(flags, queued, x0, across0, channel_gain, up, down, picks, compact)
    second = call(
        final_kernel,
        sequence,
        "svvhvhhvvvv",
        "h",
        (3_000_000_000, 11_000_000, 1_000_000),
        [message_buf, *weight_bufs, sequence_buf, sems(1), weight_sems, sems(GROUPS)],
    )(flags, queued, x1, across1, channel_gain, up, down, picks, compact, places, other)
    return first[None], second[None]


def solution(mesh):
    placed = (
        P("section", "seq", None),
        P("seq", None),
        P("section", None),
        P("section", "seq", None, None),
        P("section", "seq", None, None),
        P("section", None),
        P("section", None, None, None),
        P("section", None, None, None),
    )
    return jax.shard_map(
        per_device,
        mesh=mesh,
        in_specs=placed,
        out_specs=(P("section", "seq", None), P("section", "seq", None)),
        check_vma=False,
    )
```

```python
import functools

import jax
import jax.numpy as jnp
from jax import lax
from jax.experimental import pallas as pl
from jax.experimental.pallas import tpu as pltpu
from jax.sharding import PartitionSpec as P

EPS = 1e-05
LONG = 20_000_000_000
D = 1536
HALF = D // 2
BLK = 256
DEV = 64
GROUPS = 4
WIDTH = D // GROUPS
BF = jnp.bfloat16
F32 = jnp.float32


def call(kernel, out_shape, inputs, scratch, cost, flags=None, near=(), mib=32):
    outs = out_shape if isinstance(out_shape, tuple) else (out_shape,)
    held = pl.BlockSpec(memory_space=pl.ANY)
    nearby = pl.BlockSpec(memory_space=pltpu.VMEM)
    scalars = [] if flags is None else [pl.BlockSpec(memory_space=pltpu.SMEM)]
    flops, bytes_accessed, transcendentals = cost
    results = pl.pallas_call(
        kernel,
        out_shape=outs,
        in_specs=scalars + [nearby if n in near else held for n in range(len(inputs))],
        out_specs=[held] * len(outs),
        scratch_shapes=scratch,
        cost_estimate=pl.CostEstimate(
            flops=flops, bytes_accessed=bytes_accessed, transcendentals=transcendentals
        ),
        compiler_params=pltpu.CompilerParams(vmem_limit_bytes=mib * 1024 * 1024),
    )(
        *([] if flags is None else [flags]),
        *[
            pltpu.with_memory_space_constraint(v, pltpu.VMEM) if n in near else v
            for n, v in enumerate(inputs)
        ],
    )
    return results if isinstance(out_shape, tuple) else results[0]


def hbm(value):
    return pltpu.with_memory_space_constraint(value, pltpu.HBM)


class Copies:
    def __init__(self, sems):
        self.sems, self.made = sems, []

    def start(self, source, target):
        copy = pltpu.make_async_copy(source, target, self.sems.at[len(self.made)])
        copy.start()
        self.made.append([copy, False])
        return len(self.made) - 1

    def wait(self, *which):
        for n in which or range(len(self.made)):
            if not self.made[n][1]:
                self.made[n][0].wait()
                self.made[n][1] = True


def columns_of(g):
    return pl.ds(g * WIDTH, WIDTH)


def dot(a, b):
    return jnp.dot(a, b, preferred_element_type=F32)


def onehot(rows, cols, hit):
    r = lax.broadcasted_iota(jnp.int32, (rows, cols), 0)
    c = lax.broadcasted_iota(jnp.int32, (rows, cols), 1)
    return jnp.where(hit(r, c), 1.0, 0.0).astype(BF)


def packed_at(r, j, c, h, b):
    return (((r >> 3) * 4 + 2 * c + (r & 1)) == j) & (((r >> 1) & 3) == 2 * h + b)


def pack(c, h, b):
    return onehot(2 * BLK, BLK, lambda r, j: packed_at(r, j, c, h, b))


def whole_at(r, j, b):
    return (((r >> 3) * 4 + (r & 3)) == j) & (((r >> 2) & 1) == b)


def unpack_compact(h):
    return onehot(
        BLK, 2 * BLK, lambda q, r: r == ((q & 127) >> 1) * 8 + 4 * h + 2 * (q >> 7) + (q & 1)
    )


def pick(c):
    return onehot(BLK // 2, BLK, lambda q, j: j == (q >> 1) * 4 + 2 * c + (q & 1))


def place(c):
    return onehot(BLK, BLK // 2, lambda j, q: j == (q >> 1) * 4 + 2 * c + (q & 1))


def normalize(values, gain):
    scale = lax.rsqrt(jnp.mean(values * values, axis=-1, keepdims=True) + EPS)
    return (values * scale * gain).astype(BF)


def packed_part(packs, mixed):
    total = None
    for b in range(2):
        for h in range(2):
            term = dot(packs(h, b), mixed[b][:, h * HALF : (h + 1) * HALF])
            total = term if total is None else total + term
    return total.astype(BF).reshape(-1, 8, HALF)


def first_kernel(x_ref, gain_ref, factor_ref, out_ref, x_buf, gain_buf, factor_buf, out_buf, sems):
    copies = Copies(sems)
    rows = [pl.ds(b * BLK, BLK) for b in range(2)]
    loads = [
        copies.start(x_ref.at[rows[0]], x_buf.at[rows[0]]),
        copies.start(gain_ref, gain_buf),
        copies.start(factor_ref, factor_buf),
        copies.start(x_ref.at[rows[1]], x_buf.at[rows[1]]),
    ]
    packs = [onehot(2 * BLK, BLK, lambda r, j: whole_at(r, j, b)) for b in range(2)]
    mixed = []
    for b in range(2):
        copies.wait(loads[3 * b], loads[1], loads[2])
        normed = normalize(x_buf[rows[b], :].astype(F32), gain_buf[...])
        mixed.append(dot(factor_buf[b], normed).astype(BF))
    for g in range(GROUPS):
        part = columns_of(g)
        at = slice(g * WIDTH, (g + 1) * WIDTH)
        total = dot(packs[0], mixed[0][:, at]) + dot(packs[1], mixed[1][:, at])
        out_buf[:, :, part] = total.astype(BF).reshape(DEV, 8, WIDTH)
        copies.start(out_buf.at[:, :, part], out_ref.at[:, :, part])
    copies.wait()


def spread_kernel(cross_ref, whole_ref, out_ref, cross_buf, whole_buf, out_buf, sems):
    copies = Copies(sems)
    copies.start(cross_ref, cross_buf)
    copies.wait()
    n = 2 * BLK
    row = lax.broadcasted_iota(jnp.int32, (n, n), 0)
    col = lax.broadcasted_iota(jnp.int32, (n, n), 1)
    cross = cross_buf[...].reshape(n, 128)

    def spread(rows, columns, mask):
        full = dot(dot(onehot(n, n, rows), cross).astype(BF), onehot(128, n, columns))
        return jnp.where(((row ^ col) & mask) == 0, full, 0.0).astype(BF)

    whole_buf[...] = spread(
        lambda r, k: k == (r & 3) * 128 + (r >> 3) * 2 + ((r >> 2) & 1),
        lambda m, k: m == (k >> 3) * 2 + ((k >> 2) & 1),
        3,
    )
    copies.start(whole_buf, whole_ref)
    for c in range(2):
        out_buf[c] = spread(
            lambda r, k: k == (2 * c + (r & 1)) * 128 + (r >> 3) * 2 + ((r >> 1) & 1),
            lambda m, k: m == (k >> 3) * 2 + ((k >> 1) & 1),
            5,
        )
    copies.start(out_buf, out_ref)
    copies.wait()


def cross_kernel(c, spread_ref, r_ref, out_ref, spread_buf, out_buf, sems):
    copies = Copies(sems)
    copies.start(spread_ref if c is None else spread_ref.at[c], spread_buf)
    copies.wait()
    for g in range(out_ref.shape[2] // WIDTH):
        part = columns_of(g)
        total = dot(spread_buf[...], r_ref[:, :, part].reshape(2 * BLK, WIDTH))
        out_buf[:, :, part] = total.astype(BF).reshape(DEV, 8, WIDTH)
        copies.start(out_buf.at[:, :, part], out_ref.at[:, :, part])
    copies.wait()


def gelu(hidden):
    value = hidden.astype(BF)
    half = value * BF(0.5)
    inner = value * (BF(0.7978845608028654) + BF(0.7978845608028654 * 0.044715) * (value * value))
    return half + half * jnp.tanh(inner)


def channel_rows(residual, gain, up, down, store):
    normed = normalize(residual, gain)
    for g in range(GROUPS):
        part = slice(g * WIDTH, (g + 1) * WIDTH)
        act = gelu(dot(normed[:, part], up(g)))
        store(g, part, (residual[:, part] + dot(act, down(g))).astype(BF))


def weight_loads(copies, up_ref, down_ref, up_buf, down_buf):
    loads = [
        (
            copies.start(up_ref.at[g], up_buf.at[g]),
            copies.start(down_ref.at[g], down_buf.at[g]),
        )
        for g in range(GROUPS)
    ]

    def up(g):
        copies.wait(loads[g][0])
        return up_buf[g]

    def down(g):
        copies.wait(loads[g][1])
        return down_buf[g]

    return up, down


def middle_kernel(
    flag_ref,
    x_ref,
    across_ref,
    channel_ref,
    up_ref,
    down_ref,
    queued_ref,
    gain_ref,
    factor_ref,
    first_ref,
    entering_ref,
    mixed_ref,
    out_ref,
    x_buf,
    channel_buf,
    up_buf,
    down_buf,
    gain_buf,
    factor_buf,
    first_buf,
    entering_buf,
    mixed_buf,
    out_buf,
    sems,
    queued_sem,
):
    copies = Copies(sems)
    channel_load = copies.start(channel_ref, channel_buf)
    rows = [pl.ds(b * BLK, BLK) for b in range(2)]
    x_loads = [copies.start(x_ref.at[rows[b]], x_buf.at[rows[b]]) for b in range(2)]
    up, down = weight_loads(copies, up_ref, down_ref, up_buf, down_buf)
    late = [copies.start(gain_ref, gain_buf), copies.start(factor_ref, factor_buf)]
    queued = pltpu.make_async_copy(queued_ref, entering_buf, queued_sem.at[0])
    last = flag_ref[0] == 1

    @pl.when(last)
    def _():
        queued.start()

    unpacks = [onehot(BLK, 2 * BLK, lambda j, r: whole_at(r, j, b)) for b in range(2)]
    residuals = [[], []]
    for g in range(GROUPS):
        packed = across_ref[:, :, columns_of(g)].reshape(2 * BLK, WIDTH)
        for b in range(2):
            residuals[b].append(dot(unpacks[b], packed))
    copies.wait(channel_load)
    for b in range(2):

        def store(g, part, value):
            first_buf[rows[b], part] = value

        copies.wait(x_loads[b])
        residual = x_buf[rows[b], :].astype(F32) + jnp.concatenate(residuals[b], axis=1)
        channel_rows(residual, channel_buf[...], up, down, store)
        copies.start(first_buf.at[rows[b]], first_ref.at[rows[b]])

    @pl.when(last)
    def _():
        queued.wait()

    @pl.when(jnp.logical_not(last))
    def _():
        entering_buf[...] = first_buf[...]

    copies.wait(*late)
    mixed = []
    for b in range(2):
        copies.start(entering_buf.at[rows[b]], entering_ref.at[rows[b]])
        normed = normalize(entering_buf[rows[b], :].astype(F32), gain_buf[...])
        mixed.append(dot(factor_buf[b], normed).astype(BF))
        mixed_buf[rows[b], :] = mixed[b]
        copies.start(mixed_buf.at[rows[b]], mixed_ref.at[rows[b]])
    for n in range(2):
        part = slice(n * BLK, (n + 1) * BLK)
        devices = pl.ds(n * (DEV // 2), DEV // 2)
        out_buf[devices] = packed_part(lambda h, b: pack(0, h, b)[part], mixed)
        copies.start(out_buf.at[devices], out_ref.at[devices])
    copies.wait()


def remainder_kernel(
    entering_ref,
    mixed_ref,
    kept0_ref,
    kept1_ref,
    out_ref,
    entering_buf,
    mixed_buf,
    kept_buf,
    out_buf,
    sems,
):
    copies = Copies(sems)
    copies.start(entering_ref, entering_buf)
    copies.start(mixed_ref, mixed_buf)
    copies.wait(0)
    for c, kept_ref in enumerate((kept0_ref, kept1_ref)):
        for b in range(2):
            rows = pl.ds(b * (BLK // 2), BLK // 2)
            kept = dot(pick(c), entering_buf[b * BLK : (b + 1) * BLK, :])
            kept_buf[c, rows, :] = kept.astype(BF)
        copies.start(kept_buf.at[c], kept_ref)
    copies.wait(1)
    mixed = [mixed_buf[b * BLK : (b + 1) * BLK, :] for b in range(2)]
    out_buf[...] = packed_part(functools.partial(pack, 1), mixed)
    copies.start(out_buf, out_ref)
    copies.wait()


def last_kernel(
    x_ref,
    across_ref,
    channel_ref,
    up_ref,
    down_ref,
    *rest,
):
    whole = len(rest) > 7
    if whole:
        other_ref, out_ref, x_buf, channel_buf, up_buf, down_buf, other_buf, out_buf, sems = rest
    else:
        out_ref, x_buf, channel_buf, up_buf, down_buf, out_buf, sems = rest
    copies = Copies(sems)
    loads = [
        copies.start(x_ref, x_buf),
        copies.start(channel_ref, channel_buf),
    ]
    up, down = weight_loads(copies, up_ref, down_ref, up_buf, down_buf)
    if whole:
        other = copies.start(other_ref, other_buf)

    def store(g, part, value):
        if whole:
            copies.wait(other)
            for b in range(2):
                rows = slice(b * (BLK // 2), (b + 1) * (BLK // 2))
                joined = dot(places[0], other_buf[rows, part]) + dot(places[1], value[rows])
                out_buf[b * BLK : (b + 1) * BLK, part] = joined.astype(BF)
        else:
            out_buf[:, part] = value
        copies.start(out_buf.at[:, columns_of(g)], out_ref.at[:, columns_of(g)])

    places = [place(c) for c in range(2)] if whole else None
    compact = [unpack_compact(h) for h in range(2)]
    copies.wait(*loads)
    packed = across_ref[...].reshape(2 * BLK, HALF)
    across = jnp.concatenate([dot(compact[h], packed) for h in range(2)], axis=1)
    channel_rows(x_buf[...].astype(F32) + across, channel_buf[...], up, down, store)
    copies.wait()


def pass_kernel(value_ref, other_ref, out_ref):
    pass


def after(value, other, near=False):
    return pl.pallas_call(
        pass_kernel,
        out_shape=jax.ShapeDtypeStruct(value.shape, value.dtype),
        in_specs=[
            pl.BlockSpec(memory_space=pl.ANY),
            pl.BlockSpec(memory_space=pltpu.VMEM if near else pl.ANY),
        ],
        out_specs=pl.BlockSpec(memory_space=pl.ANY),
        input_output_aliases={0: 0},
        cost_estimate=pl.CostEstimate(flops=LONG, bytes_accessed=0, transcendentals=0),
    )(value, pltpu.with_memory_space_constraint(other, pltpu.VMEM) if near else other)


def shape(*dims):
    return jax.ShapeDtypeStruct(dims, BF)


def exchange(value):
    return lax.all_to_all(hbm(value), "seq", split_axis=0, concat_axis=0, tiled=True)


def per_device(arriving, queued, norm_gain, block_factor, cross_factor, channel_gain, up, down):
    section = lax.axis_index("section")
    count = lax.axis_size("section")
    flags = jnp.full((1,), section == count - 1, jnp.int32)
    x = arriving[0]
    factor, cross, up, down = block_factor[0], cross_factor[0], up[0], down[0]
    held_x, held_factor, held_gain = hbm(x), hbm(factor), hbm(norm_gain)
    cross, up, down, queued, channel_gain = (
        hbm(v) for v in (cross, up, down, queued, channel_gain)
    )

    def ahead(value):
        return lax.ppermute(value, "section", [(s, (s + 1) % count) for s in range(count)])

    def behind(value):
        return lax.ppermute(value, "section", [((s + 1) % count, s) for s in range(count)])

    message, both = shape(DEV, 8, HALF), shape(DEV, 8, D)
    sequence, part_rows = shape(2 * BLK, D), shape(BLK, D)
    far = pltpu.HBM(sequence.shape, BF)

    def buf(value):
        return pltpu.VMEM(value.shape, value.dtype)

    def sems(n):
        return pltpu.SemaphoreType.DMA((n,))

    sent = call(
        first_kernel,
        both,
        [held_x, held_gain, held_factor],
        [buf(x), buf(norm_gain), buf(factor), buf(both), sems(8)],
        (2_000_000_000, 4_000_000, 0),
    )
    columns = exchange(sent)
    square = shape(2 * BLK, 2 * BLK)
    whole, spread = call(
        spread_kernel,
        (square, shape(2, 2 * BLK, 2 * BLK)),
        [cross],
        [buf(cross), buf(square), buf(shape(2, 2 * BLK, 2 * BLK)), sems(3)],
        (600_000_000, 5_000_000, 0),
    )
    next_gain, next_factor = behind(norm_gain), behind(factor)

    out = call(
        functools.partial(cross_kernel, None),
        both,
        [whole, columns],
        [buf(square), buf(both), sems(5)],
        (800_000_000, 4_000_000, 0),
        near=(1,),
        mib=16,
    )
    across = exchange(out)

    first, entering, mixed, sent0 = call(
        middle_kernel,
        (sequence, far, far, message),
        [held_x, across, channel_gain, up, down, queued, next_gain, next_factor],
        [
            buf(x),
            buf(channel_gain),
            buf(up),
            buf(down),
            buf(norm_gain),
            buf(factor),
            buf(x),
            buf(x),
            buf(x),
            buf(message),
            sems(21),
            sems(1),
        ],
        (7_000_000_000, 18_000_000, 2_000_000),
        flags,
        near=(1,),
    )
    columns0 = exchange(sent0)
    kept0, kept1, sent1 = call(
        remainder_kernel,
        (part_rows, part_rows, message),
        [entering, mixed],
        [buf(x), buf(x), buf(shape(2, BLK, D)), buf(message), sems(5)],
        (1_000_000_000, 5_000_000, 0),
    )
    x0 = ahead(kept0)
    columns0, x0 = lax.optimization_barrier((columns0, x0))
    columns0, sent1 = lax.optimization_barrier((columns0, sent1))
    columns0 = ahead(columns0)
    columns1 = exchange(sent1)

    def crossed(c, value):
        return call(
            functools.partial(cross_kernel, c),
            message,
            [spread, value],
            [buf(square), buf(message), sems(3)],
            (LONG, 2_000_000, 0),
            near=(1,),
            mib=12,
        )

    across0 = exchange(after(crossed(0, columns0), columns1))
    columns1 = ahead(columns1)
    kept1, columns1 = lax.optimization_barrier((kept1, columns1))
    x1 = ahead(kept1)
    across1 = exchange(after(crossed(1, columns1), across0, True))
    bufs = [buf(part_rows), buf(channel_gain), buf(up), buf(down)]
    other = call(
        last_kernel,
        pltpu.HBM(part_rows.shape, BF),
        [x0, across0, channel_gain, up, down],
        [*bufs, buf(part_rows), sems(14)],
        (2_500_000_000, 10_000_000, 1_000_000),
        near=(1,),
    )
    second = call(
        last_kernel,
        sequence,
        [hbm(x1), across1, channel_gain, up, down, hbm(other)],
        [*bufs, buf(part_rows), buf(sequence), sems(15)],
        (3_000_000_000, 11_000_000, 1_000_000),
        near=(1,),
    )
    return first.reshape(1, *x.shape), second.reshape(1, *x.shape)


def solution(mesh):
    placed = (
        P("section", "seq", None),
        P("seq", None),
        P("section", None),
        P("section", "seq", None, None),
        P("section", "seq", None, None),
        P("section", None),
        P("section", None, None, None),
        P("section", None, None, None),
    )
    return jax.shard_map(
        per_device,
        mesh=mesh,
        in_specs=placed,
        out_specs=(P("section", "seq", None), P("section", "seq", None)),
        check_vma=False,
    )
```

```python
import functools

import jax
import jax.numpy as jnp
from jax import lax
from jax.experimental import pallas as pl
from jax.experimental.pallas import tpu as pltpu
from jax.sharding import PartitionSpec as P

EPS = 1e-05
LONG = 20_000_000_000
D = 1536
HALF = D // 2
BLK = 256
DEV = 64
GROUPS = 4
WIDTH = D // GROUPS
BF = jnp.bfloat16
F32 = jnp.float32


def call(kernel, out_shape, inputs, scratch, cost, flags=None, near=(), mib=32):
    outs = out_shape if isinstance(out_shape, tuple) else (out_shape,)
    held = pl.BlockSpec(memory_space=pl.ANY)
    nearby = pl.BlockSpec(memory_space=pltpu.VMEM)
    scalars = [] if flags is None else [pl.BlockSpec(memory_space=pltpu.SMEM)]
    flops, bytes_accessed, transcendentals = cost
    results = pl.pallas_call(
        kernel,
        out_shape=outs,
        in_specs=scalars + [nearby if n in near else held for n in range(len(inputs))],
        out_specs=[held] * len(outs),
        scratch_shapes=scratch,
        cost_estimate=pl.CostEstimate(
            flops=flops, bytes_accessed=bytes_accessed, transcendentals=transcendentals
        ),
        compiler_params=pltpu.CompilerParams(vmem_limit_bytes=mib * 1024 * 1024),
    )(
        *([] if flags is None else [flags]),
        *[
            pltpu.with_memory_space_constraint(v, pltpu.VMEM) if n in near else v
            for n, v in enumerate(inputs)
        ],
    )
    return results if isinstance(out_shape, tuple) else results[0]


def hbm(value):
    return pltpu.with_memory_space_constraint(value, pltpu.HBM)


class Copies:
    def __init__(self, sems):
        self.sems, self.made = sems, []

    def start(self, source, target):
        copy = pltpu.make_async_copy(source, target, self.sems.at[len(self.made)])
        copy.start()
        self.made.append([copy, False])
        return len(self.made) - 1

    def wait(self, *which):
        for n in which or range(len(self.made)):
            if not self.made[n][1]:
                self.made[n][0].wait()
                self.made[n][1] = True


def columns_of(g):
    return pl.ds(g * WIDTH, WIDTH)


def dot(a, b):
    return jnp.dot(a, b, preferred_element_type=F32)


def onehot(rows, cols, hit):
    r = lax.broadcasted_iota(jnp.int32, (rows, cols), 0)
    c = lax.broadcasted_iota(jnp.int32, (rows, cols), 1)
    return jnp.where(hit(r, c), 1.0, 0.0).astype(BF)


def packed_at(r, j, c, h, b):
    return (((r >> 3) * 4 + 2 * c + (r & 1)) == j) & (((r >> 1) & 3) == 2 * h + b)


def pack(c, h, b):
    return onehot(2 * BLK, BLK, lambda r, j: packed_at(r, j, c, h, b))


def whole_at(r, j, b):
    return (((r >> 3) * 4 + (r & 3)) == j) & (((r >> 2) & 1) == b)


def unpack_compact(h):
    return onehot(
        BLK, 2 * BLK, lambda q, r: r == ((q & 127) >> 1) * 8 + 4 * h + 2 * (q >> 7) + (q & 1)
    )


def pick(c):
    return onehot(BLK // 2, BLK, lambda q, j: j == (q >> 1) * 4 + 2 * c + (q & 1))


def place(c):
    return onehot(BLK, BLK // 2, lambda j, q: j == (q >> 1) * 4 + 2 * c + (q & 1))


def normalize(values, gain):
    scale = lax.rsqrt(jnp.mean(values * values, axis=-1, keepdims=True) + EPS)
    return (values * scale * gain).astype(BF)


def packed_part(packs, mixed):
    total = None
    for b in range(2):
        for h in range(2):
            term = dot(packs(h, b), mixed[b][:, h * HALF : (h + 1) * HALF])
            total = term if total is None else total + term
    return total.astype(BF).reshape(-1, 8, HALF)


def first_kernel(x_ref, gain_ref, factor_ref, out_ref, x_buf, gain_buf, factor_buf, out_buf, sems):
    copies = Copies(sems)
    rows = [pl.ds(b * BLK, BLK) for b in range(2)]
    loads = [
        copies.start(x_ref.at[rows[0]], x_buf.at[rows[0]]),
        copies.start(gain_ref, gain_buf),
        copies.start(factor_ref, factor_buf),
        copies.start(x_ref.at[rows[1]], x_buf.at[rows[1]]),
    ]
    packs = [onehot(2 * BLK, BLK, lambda r, j: whole_at(r, j, b)) for b in range(2)]
    mixed = []
    for b in range(2):
        copies.wait(loads[3 * b], loads[1], loads[2])
        normed = normalize(x_buf[rows[b], :].astype(F32), gain_buf[...])
        mixed.append(dot(factor_buf[b], normed).astype(BF))
    for g in range(GROUPS):
        part = columns_of(g)
        at = slice(g * WIDTH, (g + 1) * WIDTH)
        total = dot(packs[0], mixed[0][:, at]) + dot(packs[1], mixed[1][:, at])
        out_buf[:, :, part] = total.astype(BF).reshape(DEV, 8, WIDTH)
        copies.start(out_buf.at[:, :, part], out_ref.at[:, :, part])
    copies.wait()


def spread_kernel(cross_ref, whole_ref, out_ref, cross_buf, whole_buf, out_buf, sems):
    copies = Copies(sems)
    copies.start(cross_ref, cross_buf)
    copies.wait()
    n = 2 * BLK
    row = lax.broadcasted_iota(jnp.int32, (n, n), 0)
    col = lax.broadcasted_iota(jnp.int32, (n, n), 1)
    cross = cross_buf[...].reshape(n, 128)

    def spread(rows, columns, mask):
        full = dot(dot(onehot(n, n, rows), cross).astype(BF), onehot(128, n, columns))
        return jnp.where(((row ^ col) & mask) == 0, full, 0.0).astype(BF)

    whole_buf[...] = spread(
        lambda r, k: k == (r & 3) * 128 + (r >> 3) * 2 + ((r >> 2) & 1),
        lambda m, k: m == (k >> 3) * 2 + ((k >> 2) & 1),
        3,
    )
    copies.start(whole_buf, whole_ref)
    for c in range(2):
        out_buf[c] = spread(
            lambda r, k: k == (2 * c + (r & 1)) * 128 + (r >> 3) * 2 + ((r >> 1) & 1),
            lambda m, k: m == (k >> 3) * 2 + ((k >> 1) & 1),
            5,
        )
    copies.start(out_buf, out_ref)
    copies.wait()


def cross_kernel(c, spread_ref, r_ref, out_ref, spread_buf, out_buf, sems):
    copies = Copies(sems)
    if c is not None:
        copies.start(spread_ref.at[c], spread_buf)
        copies.wait()
        spread_ref = spread_buf
    for g in range(out_ref.shape[2] // WIDTH):
        part = columns_of(g)
        total = dot(spread_ref[...], r_ref[:, :, part].reshape(2 * BLK, WIDTH))
        out_buf[:, :, part] = total.astype(BF).reshape(DEV, 8, WIDTH)
        copies.start(out_buf.at[:, :, part], out_ref.at[:, :, part])
    copies.wait()


def gelu(hidden):
    value = hidden.astype(BF)
    half = value * BF(0.5)
    inner = value * (BF(0.7978845608028654) + BF(0.7978845608028654 * 0.044715) * (value * value))
    return half + half * jnp.tanh(inner)


def channel_rows(residual, gain, up, down, store):
    normed = normalize(residual, gain)
    for g in range(GROUPS):
        part = slice(g * WIDTH, (g + 1) * WIDTH)
        act = gelu(dot(normed[:, part], up(g)))
        store(g, part, (residual[:, part] + dot(act, down(g))).astype(BF))


def weight_loads(copies, up_ref, down_ref, up_buf, down_buf):
    loads = {}

    def start(g):
        if g < GROUPS and g not in loads:
            loads[g] = (
                copies.start(up_ref.at[g], up_buf.at[g]),
                copies.start(down_ref.at[g], down_buf.at[g]),
            )

    start(0)
    start(1)

    def up(g):
        start(g + 2)
        copies.wait(loads[g][0])
        return up_buf[g]

    def down(g):
        copies.wait(loads[g][1])
        return down_buf[g]

    return up, down, start


def middle_kernel(
    flag_ref,
    x_ref,
    across_ref,
    channel_ref,
    up_ref,
    down_ref,
    queued_ref,
    gain_ref,
    factor_ref,
    first_ref,
    entering_ref,
    mixed_ref,
    kept_ref,
    out_ref,
    x_buf,
    channel_buf,
    up_buf,
    down_buf,
    queued_buf,
    gain_buf,
    factor_buf,
    first_buf,
    entering_buf,
    mixed_buf,
    kept_buf,
    out_buf,
    sems,
):
    copies = Copies(sems)
    rows = [pl.ds(b * BLK, BLK) for b in range(2)]
    x_loads = [copies.start(x_ref.at[rows[0]], x_buf.at[rows[0]])]
    channel_load = copies.start(channel_ref, channel_buf)
    up, down, start = weight_loads(copies, up_ref, down_ref, up_buf, down_buf)
    x_loads.append(copies.start(x_ref.at[rows[1]], x_buf.at[rows[1]]))
    for g in range(2, GROUPS):
        start(g)
    late = [
        copies.start(gain_ref, gain_buf),
        copies.start(factor_ref, factor_buf),
        copies.start(queued_ref, queued_buf),
    ]
    unpacks = [onehot(BLK, 2 * BLK, lambda j, r: whole_at(r, j, b)) for b in range(2)]
    packs = [[pack(0, h, b) for h in range(2)] for b in range(2)]
    picked = pick(0)
    last = flag_ref[0] == 1
    residuals = [[], []]
    for g in range(GROUPS):
        packed = across_ref[:, :, columns_of(g)].reshape(2 * BLK, WIDTH)
        for b in range(2):
            residuals[b].append(dot(unpacks[b], packed))
    copies.wait(channel_load)
    mixed = []
    for b in range(2):

        def store(g, part, value):
            first_buf[rows[b], part] = value

        copies.wait(x_loads[b])
        residual = x_buf[rows[b], :].astype(F32) + jnp.concatenate(residuals[b], axis=1)
        channel_rows(residual, channel_buf[...], up, down, store)
        if b == 0:
            copies.wait(*late)
        copies.start(first_buf.at[rows[b]], first_ref.at[rows[b]])
        entering = jnp.where(last, queued_buf[rows[b], :], first_buf[rows[b], :])
        entering_buf[rows[b], :] = entering
        copies.start(entering_buf.at[rows[b]], entering_ref.at[rows[b]])
        half = pl.ds(b * (BLK // 2), BLK // 2)
        kept_buf[half, :] = dot(picked, entering).astype(BF)
        mixed.append(dot(factor_buf[b], normalize(entering.astype(F32), gain_buf[...])).astype(BF))
        mixed_buf[rows[b], :] = mixed[b]
        copies.start(mixed_buf.at[rows[b]], mixed_ref.at[rows[b]])
    copies.start(kept_buf, kept_ref)
    for n in range(2):
        part = slice(n * BLK, (n + 1) * BLK)
        devices = pl.ds(n * (DEV // 2), DEV // 2)
        out_buf[devices] = packed_part(lambda h, b: packs[b][h][part], mixed)
        copies.start(out_buf.at[devices], out_ref.at[devices])
    copies.wait()


def remainder_kernel(
    entering_ref, mixed_ref, kept_ref, out_ref, entering_buf, mixed_buf, kept_buf, out_buf, sems
):
    copies = Copies(sems)
    copies.start(mixed_ref, mixed_buf)
    copies.start(entering_ref, entering_buf)
    copies.wait(0)
    mixed = [mixed_buf[b * BLK : (b + 1) * BLK, :] for b in range(2)]
    out_buf[...] = packed_part(functools.partial(pack, 1), mixed)
    copies.start(out_buf, out_ref)
    copies.wait(1)
    for b in range(2):
        rows = pl.ds(b * (BLK // 2), BLK // 2)
        kept = dot(pick(1), entering_buf[b * BLK : (b + 1) * BLK, :])
        kept_buf[rows, :] = kept.astype(BF)
    copies.start(kept_buf, kept_ref)
    copies.wait()


def last_kernel(
    x_ref,
    across_ref,
    channel_ref,
    up_ref,
    down_ref,
    *rest,
):
    whole = len(rest) > 7
    if whole:
        other_ref, out_ref, x_buf, channel_buf, up_buf, down_buf, other_buf, out_buf, sems = rest
    else:
        out_ref, x_buf, channel_buf, up_buf, down_buf, out_buf, sems = rest
    copies = Copies(sems)
    loads = [
        copies.start(x_ref, x_buf),
        copies.start(channel_ref, channel_buf),
    ]
    up, down, start = weight_loads(copies, up_ref, down_ref, up_buf, down_buf)
    if whole:
        other = copies.start(other_ref, other_buf)

    def store(g, part, value):
        if whole:
            copies.wait(other)
            for b in range(2):
                rows = slice(b * (BLK // 2), (b + 1) * (BLK // 2))
                joined = dot(places[0], other_buf[rows, part]) + dot(places[1], value[rows])
                out_buf[b * BLK : (b + 1) * BLK, part] = joined.astype(BF)
        else:
            out_buf[:, part] = value
        copies.start(out_buf.at[:, columns_of(g)], out_ref.at[:, columns_of(g)])

    places = [place(c) for c in range(2)] if whole else None
    compact = [unpack_compact(h) for h in range(2)]
    copies.wait(*loads)
    start(2)
    start(3)
    packed = across_ref[...].reshape(2 * BLK, HALF)
    across = jnp.concatenate([dot(compact[h], packed) for h in range(2)], axis=1)
    channel_rows(x_buf[...].astype(F32) + across, channel_buf[...], up, down, store)
    copies.wait()


def pass_kernel(value_ref, other_ref, out_ref):
    pass


def after(value, other, near=False):
    return pl.pallas_call(
        pass_kernel,
        out_shape=jax.ShapeDtypeStruct(value.shape, value.dtype),
        in_specs=[
            pl.BlockSpec(memory_space=pl.ANY),
            pl.BlockSpec(memory_space=pltpu.VMEM if near else pl.ANY),
        ],
        out_specs=pl.BlockSpec(memory_space=pl.ANY),
        input_output_aliases={0: 0},
        cost_estimate=pl.CostEstimate(flops=LONG, bytes_accessed=0, transcendentals=0),
    )(value, pltpu.with_memory_space_constraint(other, pltpu.VMEM) if near else other)


def shape(*dims):
    return jax.ShapeDtypeStruct(dims, BF)


def exchange(value):
    return lax.all_to_all(hbm(value), "seq", split_axis=0, concat_axis=0, tiled=True)


def per_device(arriving, queued, norm_gain, block_factor, cross_factor, channel_gain, up, down):
    section = lax.axis_index("section")
    count = lax.axis_size("section")
    flags = jnp.full((1,), section == count - 1, jnp.int32)
    x = arriving[0]
    factor, cross, up, down = block_factor[0], cross_factor[0], up[0], down[0]
    held_x, held_factor, held_gain = hbm(x), hbm(factor), hbm(norm_gain)
    cross, up, down, queued, channel_gain = (
        hbm(v) for v in (cross, up, down, queued, channel_gain)
    )

    def ahead(value):
        return lax.ppermute(value, "section", [(s, (s + 1) % count) for s in range(count)])

    def behind(value):
        return lax.ppermute(value, "section", [((s + 1) % count, s) for s in range(count)])

    message, both = shape(DEV, 8, HALF), shape(DEV, 8, D)
    sequence, part_rows = shape(2 * BLK, D), shape(BLK, D)
    far = pltpu.HBM(sequence.shape, BF)

    def buf(value):
        return pltpu.VMEM(value.shape, value.dtype)

    def sems(n):
        return pltpu.SemaphoreType.DMA((n,))

    sent = call(
        first_kernel,
        both,
        [held_x, held_gain, held_factor],
        [buf(x), buf(norm_gain), buf(factor), buf(both), sems(8)],
        (2_000_000_000, 4_000_000, 0),
    )
    columns = exchange(sent)
    square = shape(2 * BLK, 2 * BLK)
    whole, spread = call(
        spread_kernel,
        (square, shape(2, 2 * BLK, 2 * BLK)),
        [cross],
        [buf(cross), buf(square), buf(shape(2, 2 * BLK, 2 * BLK)), sems(3)],
        (600_000_000, 5_000_000, 0),
    )
    next_gain, next_factor = behind(norm_gain), behind(factor)

    out = call(
        functools.partial(cross_kernel, None),
        both,
        [whole, columns],
        [buf(square), buf(both), sems(5)],
        (800_000_000, 4_000_000, 0),
        near=(0, 1),
        mib=16,
    )
    across = exchange(out)

    first, entering, mixed, kept0, sent0 = call(
        middle_kernel,
        (sequence, far, far, part_rows, message),
        [held_x, across, channel_gain, up, down, queued, next_gain, next_factor],
        [
            buf(x),
            buf(channel_gain),
            buf(up),
            buf(down),
            buf(x),
            buf(norm_gain),
            buf(factor),
            buf(x),
            buf(x),
            buf(x),
            buf(part_rows),
            buf(message),
            sems(23),
        ],
        (7_000_000_000, 18_000_000, 2_000_000),
        flags,
        near=(1,),
    )
    columns0 = exchange(sent0)
    x0 = ahead(kept0)
    kept1, sent1 = call(
        remainder_kernel,
        (part_rows, message),
        [entering, mixed],
        [buf(x), buf(x), buf(part_rows), buf(message), sems(4)],
        (1_000_000_000, 5_000_000, 0),
    )
    columns0, x0 = lax.optimization_barrier((columns0, x0))
    columns0, sent1 = lax.optimization_barrier((columns0, sent1))
    columns0 = ahead(columns0)
    columns1 = exchange(sent1)

    def crossed(c, value):
        return call(
            functools.partial(cross_kernel, c),
            message,
            [spread, value],
            [buf(square), buf(message), sems(3)],
            (LONG, 2_000_000, 0),
            near=(1,),
            mib=12,
        )

    across0 = exchange(after(crossed(0, columns0), columns1))
    columns1 = ahead(columns1)
    kept1, columns1 = lax.optimization_barrier((kept1, columns1))
    x1 = ahead(kept1)
    across1 = exchange(after(crossed(1, columns1), across0, True))
    bufs = [buf(part_rows), buf(channel_gain), buf(up), buf(down)]
    other = call(
        last_kernel,
        pltpu.HBM(part_rows.shape, BF),
        [x0, across0, channel_gain, up, down],
        [*bufs, buf(part_rows), sems(14)],
        (2_500_000_000, 10_000_000, 1_000_000),
        near=(1,),
    )
    second = call(
        last_kernel,
        sequence,
        [hbm(x1), across1, channel_gain, up, down, hbm(other)],
        [*bufs, buf(part_rows), buf(sequence), sems(15)],
        (3_000_000_000, 11_000_000, 1_000_000),
        near=(1,),
    )
    return first.reshape(1, *x.shape), second.reshape(1, *x.shape)


def solution(mesh):
    placed = (
        P("section", "seq", None),
        P("seq", None),
        P("section", None),
        P("section", "seq", None, None),
        P("section", "seq", None, None),
        P("section", None),
        P("section", None, None, None),
        P("section", None, None, None),
    )
    return jax.shard_map(
        per_device,
        mesh=mesh,
        in_specs=placed,
        out_specs=(P("section", "seq", None), P("section", "seq", None)),
        check_vma=False,
    )
```

```python
import functools

import jax
import jax.numpy as jnp
from jax import lax
from jax.experimental import pallas as pl
from jax.experimental.pallas import tpu as pltpu
from jax.sharding import PartitionSpec as P

EPS = 1e-05
LONG = 20_000_000_000
D = 1536
HALF = D // 2
BLK = 256
DEV = 64
GROUPS = 4
WIDTH = D // GROUPS
BF = jnp.bfloat16
F32 = jnp.float32


def call(kernel, out_shape, inputs, scratch, cost, flags=None, near=(), mib=32):
    outs = out_shape if isinstance(out_shape, tuple) else (out_shape,)
    held = pl.BlockSpec(memory_space=pl.ANY)
    nearby = pl.BlockSpec(memory_space=pltpu.VMEM)
    scalars = [] if flags is None else [pl.BlockSpec(memory_space=pltpu.SMEM)]
    flops, bytes_accessed, transcendentals = cost
    results = pl.pallas_call(
        kernel,
        out_shape=outs,
        in_specs=scalars + [nearby if n in near else held for n in range(len(inputs))],
        out_specs=[held] * len(outs),
        scratch_shapes=scratch,
        cost_estimate=pl.CostEstimate(
            flops=flops, bytes_accessed=bytes_accessed, transcendentals=transcendentals
        ),
        compiler_params=pltpu.CompilerParams(vmem_limit_bytes=mib * 1024 * 1024),
    )(
        *([] if flags is None else [flags]),
        *[
            pltpu.with_memory_space_constraint(v, pltpu.VMEM) if n in near else v
            for n, v in enumerate(inputs)
        ],
    )
    return results if isinstance(out_shape, tuple) else results[0]


def hbm(value):
    return pltpu.with_memory_space_constraint(value, pltpu.HBM)


class Copies:
    def __init__(self, sems):
        self.sems, self.made = sems, []

    def start(self, source, target):
        copy = pltpu.make_async_copy(source, target, self.sems.at[len(self.made)])
        copy.start()
        self.made.append([copy, False])
        return len(self.made) - 1

    def wait(self, *which):
        for n in which or range(len(self.made)):
            if not self.made[n][1]:
                self.made[n][0].wait()
                self.made[n][1] = True


def columns_of(g):
    return pl.ds(g * WIDTH, WIDTH)


def dot(a, b):
    return jnp.dot(a, b, preferred_element_type=F32)


def onehot(rows, cols, hit):
    r = lax.broadcasted_iota(jnp.int32, (rows, cols), 0)
    c = lax.broadcasted_iota(jnp.int32, (rows, cols), 1)
    return jnp.where(hit(r, c), 1.0, 0.0).astype(BF)


def packed_at(r, j, c, h, b):
    return (((r >> 3) * 4 + 2 * c + (r & 1)) == j) & (((r >> 1) & 3) == 2 * h + b)


def pack(c, h, b):
    return onehot(2 * BLK, BLK, lambda r, j: packed_at(r, j, c, h, b))


def whole_at(r, j, b):
    return (((r >> 3) * 4 + (r & 3)) == j) & (((r >> 2) & 1) == b)


def unpack_compact(h):
    return onehot(
        BLK, 2 * BLK, lambda q, r: r == ((q & 127) >> 1) * 8 + 4 * h + 2 * (q >> 7) + (q & 1)
    )


def pick(c):
    return onehot(BLK // 2, BLK, lambda q, j: j == (q >> 1) * 4 + 2 * c + (q & 1))


def place(c):
    return onehot(BLK, BLK // 2, lambda j, q: j == (q >> 1) * 4 + 2 * c + (q & 1))


def normalize(values, gain):
    scale = lax.rsqrt(jnp.mean(values * values, axis=-1, keepdims=True) + EPS)
    return (values * scale * gain).astype(BF)


def packed_part(packs, mixed):
    total = None
    for b in range(2):
        for h in range(2):
            term = dot(packs(h, b), mixed[b][:, h * HALF : (h + 1) * HALF])
            total = term if total is None else total + term
    return total.astype(BF).reshape(-1, 8, HALF)


def first_kernel(x_ref, gain_ref, factor_ref, out_ref, x_buf, gain_buf, factor_buf, out_buf, sems):
    copies = Copies(sems)
    rows = [pl.ds(b * BLK, BLK) for b in range(2)]
    loads = [
        copies.start(x_ref.at[rows[0]], x_buf.at[rows[0]]),
        copies.start(gain_ref, gain_buf),
        copies.start(factor_ref, factor_buf),
        copies.start(x_ref.at[rows[1]], x_buf.at[rows[1]]),
    ]
    packs = [onehot(2 * BLK, BLK, lambda r, j: whole_at(r, j, b)) for b in range(2)]
    mixed = []
    for b in range(2):
        copies.wait(loads[3 * b], loads[1], loads[2])
        normed = normalize(x_buf[rows[b], :].astype(F32), gain_buf[...])
        mixed.append(dot(factor_buf[b], normed).astype(BF))
    for g in range(GROUPS):
        part = columns_of(g)
        at = slice(g * WIDTH, (g + 1) * WIDTH)
        total = dot(packs[0], mixed[0][:, at]) + dot(packs[1], mixed[1][:, at])
        out_buf[:, :, part] = total.astype(BF).reshape(DEV, 8, WIDTH)
        copies.start(out_buf.at[:, :, part], out_ref.at[:, :, part])
    copies.wait()


def spread(cross, rows, columns, mask):
    n = 2 * BLK
    row = lax.broadcasted_iota(jnp.int32, (n, n), 0)
    col = lax.broadcasted_iota(jnp.int32, (n, n), 1)
    full = dot(dot(onehot(n, n, rows), cross).astype(BF), onehot(128, n, columns))
    return jnp.where(((row ^ col) & mask) == 0, full, 0.0).astype(BF)


def spread_part(cross, c):
    return spread(
        cross,
        lambda r, k: k == (2 * c + (r & 1)) * 128 + (r >> 3) * 2 + ((r >> 1) & 1),
        lambda m, k: m == (k >> 3) * 2 + ((k >> 1) & 1),
        5,
    )


def spread_own_kernel(cross_ref, whole_ref, part_ref, cross_buf, whole_buf, part_buf, sems):
    copies = Copies(sems)
    copies.start(cross_ref, cross_buf)
    copies.wait()
    cross = cross_buf[...].reshape(2 * BLK, 128)
    whole_buf[...] = spread(
        cross,
        lambda r, k: k == (r & 3) * 128 + (r >> 3) * 2 + ((r >> 2) & 1),
        lambda m, k: m == (k >> 3) * 2 + ((k >> 2) & 1),
        3,
    )
    copies.start(whole_buf, whole_ref)
    part_buf[...] = spread_part(cross, 1)
    copies.start(part_buf, part_ref)
    copies.wait()


def spread_next_kernel(cross_ref, part_ref, cross_buf, part_buf, sems):
    copies = Copies(sems)
    copies.start(cross_ref, cross_buf)
    copies.wait()
    part_buf[...] = spread_part(cross_buf[...].reshape(2 * BLK, 128), 0)
    copies.start(part_buf, part_ref)
    copies.wait()


def cross_groups(copies, spread_ref, columns, out_ref, out_buf):
    for g in range(out_ref.shape[2] // WIDTH):
        part = columns_of(g)
        total = dot(spread_ref[...], columns(part).reshape(2 * BLK, WIDTH))
        out_buf[:, :, part] = total.astype(BF).reshape(DEV, 8, WIDTH)
        copies.start(out_buf.at[:, :, part], out_ref.at[:, :, part])


def cross_whole_kernel(spread_ref, r_ref, out_ref, out_buf, sems):
    copies = Copies(sems)
    cross_groups(copies, spread_ref, lambda part: r_ref[:, :, part], out_ref, out_buf)
    copies.wait()


def cross_first_kernel(spread_ref, r_ref, out_ref, other_ref, spread_buf, out_buf, sems):
    copies = Copies(sems)
    copies.start(spread_ref, spread_buf)
    copies.start(r_ref.at[:, 1], other_ref)
    copies.wait(0)
    cross_groups(copies, spread_buf, lambda part: r_ref[:, 0, :, part], out_ref, out_buf)
    copies.wait()


def cross_second_kernel(spread_ref, r_ref, out_ref, spread_buf, out_buf, sems):
    copies = Copies(sems)
    copies.start(spread_ref, spread_buf)
    copies.wait()
    cross_groups(copies, spread_buf, lambda part: r_ref[:, :, part], out_ref, out_buf)
    copies.wait()


def gelu(hidden):
    value = hidden.astype(BF)
    half = value * BF(0.5)
    inner = value * (BF(0.7978845608028654) + BF(0.7978845608028654 * 0.044715) * (value * value))
    return half + half * jnp.tanh(inner)


def channel_rows(residual, gain, up, down, store):
    normed = normalize(residual, gain)
    for g in range(GROUPS):
        part = slice(g * WIDTH, (g + 1) * WIDTH)
        act = gelu(dot(normed[:, part], up(g)))
        store(g, part, (residual[:, part] + dot(act, down(g))).astype(BF))


def weight_loads(copies, up_ref, down_ref, up_buf, down_buf):
    loads = {}

    def start(g):
        if g < GROUPS and g not in loads:
            loads[g] = (
                copies.start(up_ref.at[g], up_buf.at[g]),
                copies.start(down_ref.at[g], down_buf.at[g]),
            )

    start(0)
    start(1)

    def up(g):
        start(g + 2)
        copies.wait(loads[g][0])
        return up_buf[g]

    def down(g):
        copies.wait(loads[g][1])
        return down_buf[g]

    return up, down, start


def middle_kernel(
    flag_ref,
    x_ref,
    across_ref,
    channel_ref,
    up_ref,
    down_ref,
    queued_ref,
    gain_ref,
    factor_ref,
    first_ref,
    entering_ref,
    out_ref,
    x_buf,
    channel_buf,
    up_buf,
    down_buf,
    queued_buf,
    gain_buf,
    factor_buf,
    first_buf,
    entering_buf,
    out_buf,
    sems,
):
    copies = Copies(sems)
    rows = [pl.ds(b * BLK, BLK) for b in range(2)]
    x_loads = [copies.start(x_ref.at[rows[0]], x_buf.at[rows[0]])]
    channel_load = copies.start(channel_ref, channel_buf)
    up, down, start = weight_loads(copies, up_ref, down_ref, up_buf, down_buf)
    x_loads.append(copies.start(x_ref.at[rows[1]], x_buf.at[rows[1]]))
    for g in range(2, GROUPS):
        start(g)
    late = [
        copies.start(gain_ref, gain_buf),
        copies.start(factor_ref, factor_buf),
        copies.start(queued_ref, queued_buf),
    ]
    unpacks = [onehot(BLK, 2 * BLK, lambda j, r: whole_at(r, j, b)) for b in range(2)]
    last = flag_ref[0] == 1
    residuals = [[], []]
    for g in range(GROUPS):
        packed = across_ref[:, :, columns_of(g)].reshape(2 * BLK, WIDTH)
        for b in range(2):
            residuals[b].append(dot(unpacks[b], packed))
    copies.wait(channel_load)
    mixed = []
    for b in range(2):

        def store(g, part, value):
            first_buf[rows[b], part] = value

        copies.wait(x_loads[b])
        residual = x_buf[rows[b], :].astype(F32) + jnp.concatenate(residuals[b], axis=1)
        channel_rows(residual, channel_buf[...], up, down, store)
        if b == 0:
            copies.wait(*late)
        copies.start(first_buf.at[rows[b]], first_ref.at[rows[b]])
        entering = jnp.where(last, queued_buf[rows[b], :], first_buf[rows[b], :])
        entering_buf[rows[b], :] = entering
        copies.start(entering_buf.at[rows[b]], entering_ref.at[rows[b]])
        mixed.append(dot(factor_buf[b], normalize(entering.astype(F32), gain_buf[...])).astype(BF))
    for c in range(2):
        out_buf[c] = packed_part(functools.partial(pack, c), mixed)
        copies.start(out_buf.at[c], out_ref.at[:, c])
    copies.wait()


def last_rows(copies, loads, residual_of, across_ref, channel_buf, weights, store):
    up, down, start = weights
    compact = [unpack_compact(h) for h in range(2)]
    copies.wait(*loads)
    start(2)
    start(3)
    packed = across_ref[...].reshape(2 * BLK, HALF)
    across = jnp.concatenate([dot(compact[h], packed) for h in range(2)], axis=1)
    channel_rows(residual_of() + across, channel_buf[...], up, down, store)


def last_kernel(
    x_ref,
    across_ref,
    channel_ref,
    up_ref,
    down_ref,
    out_ref,
    kept_ref,
    x_buf,
    channel_buf,
    up_buf,
    down_buf,
    out_buf,
    kept_buf,
    sems,
):
    copies = Copies(sems)
    loads = [copies.start(x_ref, x_buf), copies.start(channel_ref, channel_buf)]
    weights = weight_loads(copies, up_ref, down_ref, up_buf, down_buf)

    def rows_of(c):
        picked = [dot(pick(c), x_buf[b * BLK : (b + 1) * BLK, :]) for b in range(2)]
        return jnp.concatenate(picked, axis=0)

    def store(g, part, value):
        out_buf[:, part] = value
        copies.start(out_buf.at[:, columns_of(g)], out_ref.at[:, columns_of(g)])

    last_rows(copies, loads, lambda: rows_of(0), across_ref, channel_buf, weights, store)
    kept_buf[...] = rows_of(1).astype(BF)
    copies.start(kept_buf, kept_ref)
    copies.wait()


def final_kernel(
    x_ref,
    across_ref,
    channel_ref,
    up_ref,
    down_ref,
    other_ref,
    out_ref,
    x_buf,
    channel_buf,
    up_buf,
    down_buf,
    other_buf,
    out_buf,
    sems,
):
    copies = Copies(sems)
    loads = [copies.start(x_ref, x_buf), copies.start(channel_ref, channel_buf)]
    weights = weight_loads(copies, up_ref, down_ref, up_buf, down_buf)
    other = copies.start(other_ref, other_buf)
    places = [place(c) for c in range(2)]

    def store(g, part, value):
        copies.wait(other)
        for b in range(2):
            rows = slice(b * (BLK // 2), (b + 1) * (BLK // 2))
            joined = dot(places[0], other_buf[rows, part]) + dot(places[1], value[rows])
            out_buf[b * BLK : (b + 1) * BLK, part] = joined.astype(BF)
        copies.start(out_buf.at[:, columns_of(g)], out_ref.at[:, columns_of(g)])

    last_rows(
        copies, loads, lambda: x_buf[...].astype(F32), across_ref, channel_buf, weights, store
    )
    copies.wait()


def pass_kernel(value_ref, other_ref, out_ref):
    pass


def after(value, other, near=False):
    return pl.pallas_call(
        pass_kernel,
        out_shape=jax.ShapeDtypeStruct(value.shape, value.dtype),
        in_specs=[
            pl.BlockSpec(memory_space=pl.ANY),
            pl.BlockSpec(memory_space=pltpu.VMEM if near else pl.ANY),
        ],
        out_specs=pl.BlockSpec(memory_space=pl.ANY),
        input_output_aliases={0: 0},
        cost_estimate=pl.CostEstimate(flops=LONG, bytes_accessed=0, transcendentals=0),
    )(value, pltpu.with_memory_space_constraint(other, pltpu.VMEM) if near else other)


def shape(*dims):
    return jax.ShapeDtypeStruct(dims, BF)


def exchange(value):
    return lax.all_to_all(hbm(value), "seq", split_axis=0, concat_axis=0, tiled=True)


def per_device(arriving, queued, norm_gain, block_factor, cross_factor, channel_gain, up, down):
    section = lax.axis_index("section")
    count = lax.axis_size("section")
    flags = jnp.full((1,), section == count - 1, jnp.int32)
    x = arriving[0]
    factor, cross, up, down = block_factor[0], cross_factor[0], up[0], down[0]
    held_x, held_factor, held_gain = hbm(x), hbm(factor), hbm(norm_gain)
    cross, up, down, queued, channel_gain = (
        hbm(v) for v in (cross, up, down, queued, channel_gain)
    )

    def ahead(value):
        return lax.ppermute(value, "section", [(s, (s + 1) % count) for s in range(count)])

    def behind(value):
        return lax.ppermute(value, "section", [((s + 1) % count, s) for s in range(count)])

    message, both, pair = shape(DEV, 8, HALF), shape(DEV, 8, D), shape(DEV, 2, 8, HALF)
    square = shape(2 * BLK, 2 * BLK)
    sequence, part_rows = shape(2 * BLK, D), shape(BLK, D)

    def buf(value):
        return pltpu.VMEM(value.shape, value.dtype)

    def far(value):
        return pltpu.HBM(value.shape, value.dtype)

    def sems(n):
        return pltpu.SemaphoreType.DMA((n,))

    sent = call(
        first_kernel,
        both,
        [held_x, held_gain, held_factor],
        [buf(x), buf(norm_gain), buf(factor), buf(both), sems(8)],
        (2_000_000_000, 4_000_000, 0),
    )
    columns = exchange(sent)
    whole, own_part = call(
        spread_own_kernel,
        (square, square),
        [cross],
        [buf(cross), buf(square), buf(square), sems(3)],
        (400_000_000, 3_000_000, 0),
    )
    next_gain, next_factor, next_cross = behind(norm_gain), behind(factor), behind(cross)
    out = call(
        cross_whole_kernel,
        both,
        [whole, columns],
        [buf(both), sems(4)],
        (800_000_000, 4_000_000, 0),
        near=(0, 1),
        mib=16,
    )
    across = exchange(out)
    next_part = call(
        spread_next_kernel,
        square,
        [next_cross],
        [buf(cross), buf(square), sems(2)],
        (200_000_000, 2_000_000, 0),
    )

    first, entering, sent = call(
        middle_kernel,
        (sequence, far(sequence), pair),
        [held_x, across, channel_gain, up, down, queued, next_gain, next_factor],
        [
            buf(x),
            buf(channel_gain),
            buf(up),
            buf(down),
            buf(x),
            buf(norm_gain),
            buf(factor),
            buf(x),
            buf(x),
            buf(shape(2, DEV, 8, HALF)),
            sems(20),
        ],
        (7_000_000_000, 18_000_000, 2_000_000),
        flags,
        near=(1,),
    )
    columns = exchange(sent)
    entered = ahead(entering)
    entered = after(entered, flags)
    columns, entered = lax.optimization_barrier((columns, entered))
    out0, columns1 = call(
        cross_first_kernel,
        (message, far(message)),
        [next_part, columns],
        [buf(square), buf(message), sems(4)],
        (400_000_000, 2_000_000, 0),
        near=(1,),
        mib=12,
    )
    across0 = exchange(out0)
    columns1 = ahead(columns1)
    out1 = call(
        cross_second_kernel,
        message,
        [own_part, columns1],
        [buf(square), buf(message), sems(3)],
        (LONG, 2_000_000, 0),
        near=(1,),
        mib=12,
    )
    across1 = exchange(after(out1, across0, True))
    across0 = ahead(across0)
    bufs = [buf(channel_gain), buf(up), buf(down)]
    other, kept = call(
        last_kernel,
        (far(part_rows), far(part_rows)),
        [entered, across0, channel_gain, up, down],
        [buf(sequence), *bufs, buf(part_rows), buf(part_rows), sems(15)],
        (LONG, 10_000_000, 1_000_000),
        near=(1,),
    )
    second = call(
        final_kernel,
        sequence,
        [hbm(kept), across1, channel_gain, up, down, hbm(other)],
        [buf(part_rows), *bufs, buf(part_rows), buf(sequence), sems(15)],
        (3_000_000_000, 11_000_000, 1_000_000),
        near=(1,),
    )
    return first.reshape(1, *x.shape), second.reshape(1, *x.shape)


def solution(mesh):
    placed = (
        P("section", "seq", None),
        P("seq", None),
        P("section", None),
        P("section", "seq", None, None),
        P("section", "seq", None, None),
        P("section", None),
        P("section", None, None, None),
        P("section", None, None, None),
    )
    return jax.shard_map(
        per_device,
        mesh=mesh,
        in_specs=placed,
        out_specs=(P("section", "seq", None), P("section", "seq", None)),
        check_vma=False,
    )
```

```python
import functools

import jax
import jax.numpy as jnp
from jax import lax
from jax.experimental import pallas as pl
from jax.experimental.pallas import tpu as pltpu
from jax.sharding import PartitionSpec as P

EPS = 1e-05
LONG = 20_000_000_000
D = 1536
HALF = D // 2
BLK = 256
DEV = 64
GROUPS = 4
WIDTH = D // GROUPS
BF = jnp.bfloat16
F32 = jnp.float32


def call(kernel, out_shape, inputs, scratch, cost, flags=None, near=(), mib=32):
    outs = out_shape if isinstance(out_shape, tuple) else (out_shape,)
    held = pl.BlockSpec(memory_space=pl.ANY)
    nearby = pl.BlockSpec(memory_space=pltpu.VMEM)
    scalars = [] if flags is None else [pl.BlockSpec(memory_space=pltpu.SMEM)]
    flops, bytes_accessed, transcendentals = cost
    results = pl.pallas_call(
        kernel,
        out_shape=outs,
        in_specs=scalars + [nearby if n in near else held for n in range(len(inputs))],
        out_specs=[held] * len(outs),
        scratch_shapes=scratch,
        cost_estimate=pl.CostEstimate(
            flops=flops, bytes_accessed=bytes_accessed, transcendentals=transcendentals
        ),
        compiler_params=pltpu.CompilerParams(vmem_limit_bytes=mib * 1024 * 1024),
    )(
        *([] if flags is None else [flags]),
        *[
            pltpu.with_memory_space_constraint(v, pltpu.VMEM) if n in near else v
            for n, v in enumerate(inputs)
        ],
    )
    return results if isinstance(out_shape, tuple) else results[0]


def hbm(value):
    return pltpu.with_memory_space_constraint(value, pltpu.HBM)


class Copies:
    def __init__(self, sems):
        self.sems, self.made = sems, []

    def start(self, source, target):
        copy = pltpu.make_async_copy(source, target, self.sems.at[len(self.made)])
        copy.start()
        self.made.append([copy, False])
        return len(self.made) - 1

    def wait(self, *which):
        for n in which or range(len(self.made)):
            if not self.made[n][1]:
                self.made[n][0].wait()
                self.made[n][1] = True


def columns_of(g):
    return pl.ds(g * WIDTH, WIDTH)


def dot(a, b):
    return jnp.dot(a, b, preferred_element_type=F32)


def onehot(rows, cols, hit):
    r = lax.broadcasted_iota(jnp.int32, (rows, cols), 0)
    c = lax.broadcasted_iota(jnp.int32, (rows, cols), 1)
    return jnp.where(hit(r, c), 1.0, 0.0).astype(BF)


def offsets_of(rows, c):
    return rows.reshape(DEV, 4, -1)[:, 2 * c : 2 * c + 2].reshape(BLK // 2, -1)


def normalize(values, gain):
    scale = lax.rsqrt(jnp.mean(values * values, axis=-1, keepdims=True) + EPS)
    return (values * scale * gain).astype(BF)


def first_kernel(x_ref, gain_ref, factor_ref, out_ref, x_buf, gain_buf, factor_buf, out_buf, sems):
    copies = Copies(sems)
    rows = [pl.ds(b * BLK, BLK) for b in range(2)]
    loads = [
        copies.start(x_ref.at[rows[0]], x_buf.at[rows[0]]),
        copies.start(gain_ref, gain_buf),
        copies.start(factor_ref, factor_buf),
        copies.start(x_ref.at[rows[1]], x_buf.at[rows[1]]),
    ]
    for b in range(2):
        copies.wait(loads[3 * b], loads[1], loads[2])
        normed = normalize(x_buf[rows[b], :].astype(F32), gain_buf[...])
        mixed = dot(factor_buf[b], normed).astype(BF)
        out_buf[:, b] = mixed.reshape(DEV, 4, D)
        copies.start(out_buf.at[:, b], out_ref.at[:, b])
    copies.wait()


def spread(cross, rows, columns, mask):
    n = 2 * BLK
    row = lax.broadcasted_iota(jnp.int32, (n, n), 0)
    col = lax.broadcasted_iota(jnp.int32, (n, n), 1)
    full = dot(dot(onehot(n, n, rows), cross).astype(BF), onehot(128, n, columns))
    return jnp.where(((row ^ col) & mask) == 0, full, 0.0).astype(BF)


def spread_part(cross, c):
    return spread(
        cross,
        lambda r, k: k == (2 * c + (r & 1)) * 128 + (r >> 3) * 2 + ((r >> 1) & 1),
        lambda m, k: m == (k >> 3) * 2 + ((k >> 1) & 1),
        5,
    )


def spread_own_kernel(cross_ref, whole_ref, part_ref, cross_buf, whole_buf, part_buf, sems):
    copies = Copies(sems)
    copies.start(cross_ref, cross_buf)
    copies.wait()
    cross = cross_buf[...].reshape(2 * BLK, 128)
    whole_buf[...] = spread(
        cross,
        lambda r, k: k == (r & 3) * 128 + (r >> 3) * 2 + ((r >> 2) & 1),
        lambda m, k: m == (k >> 3) * 2 + ((k >> 2) & 1),
        3,
    )
    copies.start(whole_buf, whole_ref)
    part_buf[...] = spread_part(cross, 1)
    copies.start(part_buf, part_ref)
    copies.wait()


def spread_next_kernel(cross_ref, part_ref, cross_buf, part_buf, sems):
    copies = Copies(sems)
    copies.start(cross_ref, cross_buf)
    copies.wait()
    part_buf[...] = spread_part(cross_buf[...].reshape(2 * BLK, 128), 0)
    copies.start(part_buf, part_ref)
    copies.wait()


def cross_groups(copies, spread_ref, columns, out_ref, out_buf):
    for g in range(out_ref.shape[-1] // WIDTH):
        part = (slice(None),) * (len(out_ref.shape) - 1) + (columns_of(g),)
        total = dot(spread_ref[...], columns(part).reshape(2 * BLK, WIDTH))
        out_buf[part] = total.astype(BF).reshape(out_ref.shape[:-1] + (WIDTH,))
        copies.start(out_buf.at[part], out_ref.at[part])


def cross_whole_kernel(spread_ref, r_ref, out_ref, out_buf, sems):
    copies = Copies(sems)
    cross_groups(copies, spread_ref, lambda part: r_ref[part], out_ref, out_buf)
    copies.wait()


def cross_first_kernel(spread_ref, r_ref, out_ref, other_ref, spread_buf, out_buf, sems):
    copies = Copies(sems)
    copies.start(spread_ref, spread_buf)
    copies.start(r_ref.at[:, 1], other_ref)
    copies.wait(0)
    cross_groups(copies, spread_buf, lambda part: r_ref[:, 0, :, part[-1]], out_ref, out_buf)
    copies.wait()


def cross_second_kernel(spread_ref, r_ref, out_ref, spread_buf, out_buf, sems):
    copies = Copies(sems)
    copies.start(spread_ref, spread_buf)
    copies.wait()
    cross_groups(copies, spread_buf, lambda part: r_ref[part], out_ref, out_buf)
    copies.wait()


def gelu(hidden):
    value = hidden.astype(BF)
    half = value * BF(0.5)
    inner = value * (BF(0.7978845608028654) + BF(0.7978845608028654 * 0.044715) * (value * value))
    return half + half * jnp.tanh(inner)


def channel_rows(residual, gain, up, down, store):
    normed = normalize(residual, gain)
    for g in range(GROUPS):
        part = slice(g * WIDTH, (g + 1) * WIDTH)
        act = gelu(dot(normed[:, part], up(g)))
        store(g, part, (residual[:, part] + dot(act, down(g))).astype(BF))


def weight_loads(copies, up_ref, down_ref, up_buf, down_buf):
    loads = {}

    def start(g):
        if g < GROUPS and g not in loads:
            loads[g] = (
                copies.start(up_ref.at[g], up_buf.at[g]),
                copies.start(down_ref.at[g], down_buf.at[g]),
            )

    start(0)
    start(1)

    def up(g):
        start(g + 2)
        copies.wait(loads[g][0])
        return up_buf[g]

    def down(g):
        copies.wait(loads[g][1])
        return down_buf[g]

    return up, down, start


def middle_kernel(
    flag_ref,
    x_ref,
    across_ref,
    channel_ref,
    up_ref,
    down_ref,
    queued_ref,
    gain_ref,
    factor_ref,
    first_ref,
    entering_ref,
    out_ref,
    x_buf,
    channel_buf,
    up_buf,
    down_buf,
    queued_buf,
    gain_buf,
    factor_buf,
    first_buf,
    entering_buf,
    out_buf,
    sems,
):
    copies = Copies(sems)
    rows = [pl.ds(b * BLK, BLK) for b in range(2)]
    x_loads = [copies.start(x_ref.at[rows[0]], x_buf.at[rows[0]])]
    channel_load = copies.start(channel_ref, channel_buf)
    up, down, start = weight_loads(copies, up_ref, down_ref, up_buf, down_buf)
    x_loads.append(copies.start(x_ref.at[rows[1]], x_buf.at[rows[1]]))
    for g in range(2, GROUPS):
        start(g)
    late = [
        copies.start(gain_ref, gain_buf),
        copies.start(factor_ref, factor_buf),
        copies.start(queued_ref, queued_buf),
    ]
    last = flag_ref[0] == 1
    copies.wait(channel_load)
    mixed = []
    for b in range(2):

        def store(g, part, value):
            first_buf[rows[b], part] = value

        copies.wait(x_loads[b])
        residual = x_buf[rows[b], :].astype(F32) + across_ref[:, b].reshape(BLK, D).astype(F32)
        channel_rows(residual, channel_buf[...], up, down, store)
        if b == 0:
            copies.wait(*late)
        copies.start(first_buf.at[rows[b]], first_ref.at[rows[b]])
        entering = jnp.where(last, queued_buf[rows[b], :], first_buf[rows[b], :])
        entering_buf[rows[b], :] = entering
        copies.start(entering_buf.at[rows[b]], entering_ref.at[rows[b]])
        mixed.append(dot(factor_buf[b], normalize(entering.astype(F32), gain_buf[...])).astype(BF))
    for c in range(2):
        for b in range(2):
            rows_c = mixed[b].reshape(DEV, 4, D)[:, 2 * c : 2 * c + 2]
            for h in range(2):
                first_row = 4 * h + 2 * b
                half = slice(h * HALF, (h + 1) * HALF)
                out_buf[c, :, first_row : first_row + 2, :] = rows_c[:, :, half]
        copies.start(out_buf.at[c], out_ref.at[:, c])
    copies.wait()


def last_rows(copies, loads, residual_of, across_ref, channel_buf, weights, store):
    up, down, start = weights
    copies.wait(*loads)
    start(2)
    start(3)
    halves = [
        [
            across_ref[:, 4 * h + 2 * b : 4 * h + 2 * b + 2, :].reshape(BLK // 2, HALF)
            for h in range(2)
        ]
        for b in range(2)
    ]
    across = jnp.concatenate([jnp.concatenate(halves[b], axis=1) for b in range(2)], axis=0)
    channel_rows(residual_of() + across.astype(F32), channel_buf[...], up, down, store)


def last_kernel(
    x_ref,
    across_ref,
    channel_ref,
    up_ref,
    down_ref,
    out_ref,
    kept_ref,
    x_buf,
    channel_buf,
    up_buf,
    down_buf,
    out_buf,
    kept_buf,
    sems,
):
    copies = Copies(sems)
    loads = [copies.start(x_ref, x_buf), copies.start(channel_ref, channel_buf)]
    weights = weight_loads(copies, up_ref, down_ref, up_buf, down_buf)

    def rows_of(c):
        picked = [offsets_of(x_buf[b * BLK : (b + 1) * BLK, :], c) for b in range(2)]
        return jnp.concatenate(picked, axis=0)

    def store(g, part, value):
        out_buf[:, part] = value
        copies.start(out_buf.at[:, columns_of(g)], out_ref.at[:, columns_of(g)])

    last_rows(copies, loads, lambda: rows_of(0).astype(F32), across_ref, channel_buf, weights, store)
    kept_buf[...] = rows_of(1)
    copies.start(kept_buf, kept_ref)
    copies.wait()


def final_kernel(
    x_ref,
    across_ref,
    channel_ref,
    up_ref,
    down_ref,
    other_ref,
    out_ref,
    x_buf,
    channel_buf,
    up_buf,
    down_buf,
    other_buf,
    out_buf,
    sems,
):
    copies = Copies(sems)
    loads = [copies.start(x_ref, x_buf), copies.start(channel_ref, channel_buf)]
    weights = weight_loads(copies, up_ref, down_ref, up_buf, down_buf)
    other = copies.start(other_ref, other_buf)

    def store(g, part, value):
        copies.wait(other)
        for b in range(2):
            rows = slice(b * (BLK // 2), (b + 1) * (BLK // 2))
            both = [v.reshape(DEV, 2, WIDTH) for v in (other_buf[rows, part], value[rows])]
            joined = jnp.concatenate(both, axis=1).reshape(BLK, WIDTH)
            out_buf[b * BLK : (b + 1) * BLK, part] = joined
        copies.start(out_buf.at[:, columns_of(g)], out_ref.at[:, columns_of(g)])

    last_rows(
        copies, loads, lambda: x_buf[...].astype(F32), across_ref, channel_buf, weights, store
    )
    copies.wait()


def pass_kernel(value_ref, other_ref, out_ref):
    pass


def after(value, other, near=False):
    return pl.pallas_call(
        pass_kernel,
        out_shape=jax.ShapeDtypeStruct(value.shape, value.dtype),
        in_specs=[
            pl.BlockSpec(memory_space=pl.ANY),
            pl.BlockSpec(memory_space=pltpu.VMEM if near else pl.ANY),
        ],
        out_specs=pl.BlockSpec(memory_space=pl.ANY),
        input_output_aliases={0: 0},
        cost_estimate=pl.CostEstimate(flops=LONG, bytes_accessed=0, transcendentals=0),
    )(value, pltpu.with_memory_space_constraint(other, pltpu.VMEM) if near else other)


def shape(*dims):
    return jax.ShapeDtypeStruct(dims, BF)


def exchange(value):
    return lax.all_to_all(hbm(value), "seq", split_axis=0, concat_axis=0, tiled=True)


def per_device(arriving, queued, norm_gain, block_factor, cross_factor, channel_gain, up, down):
    section = lax.axis_index("section")
    count = lax.axis_size("section")
    flags = jnp.full((1,), section == count - 1, jnp.int32)
    x = arriving[0]
    factor, cross, up, down = block_factor[0], cross_factor[0], up[0], down[0]
    held_x, held_factor, held_gain = hbm(x), hbm(factor), hbm(norm_gain)
    cross, up, down, queued, channel_gain = (
        hbm(v) for v in (cross, up, down, queued, channel_gain)
    )

    def ahead(value):
        return lax.ppermute(value, "section", [(s, (s + 1) % count) for s in range(count)])

    def behind(value):
        return lax.ppermute(value, "section", [((s + 1) % count, s) for s in range(count)])

    message, both, pair = shape(DEV, 8, HALF), shape(DEV, 2, 4, D), shape(DEV, 2, 8, HALF)
    square = shape(2 * BLK, 2 * BLK)
    sequence, part_rows = shape(2 * BLK, D), shape(BLK, D)

    def buf(value):
        return pltpu.VMEM(value.shape, value.dtype)

    def far(value):
        return pltpu.HBM(value.shape, value.dtype)

    def sems(n):
        return pltpu.SemaphoreType.DMA((n,))

    sent = call(
        first_kernel,
        both,
        [held_x, held_gain, held_factor],
        [buf(x), buf(norm_gain), buf(factor), buf(both), sems(6)],
        (2_000_000_000, 4_000_000, 0),
    )
    columns = exchange(sent)
    whole, own_part = call(
        spread_own_kernel,
        (square, square),
        [cross],
        [buf(cross), buf(square), buf(square), sems(3)],
        (400_000_000, 3_000_000, 0),
    )
    next_gain, next_factor, next_cross = behind(norm_gain), behind(factor), behind(cross)
    out = call(
        cross_whole_kernel,
        both,
        [whole, columns],
        [buf(both), sems(4)],
        (800_000_000, 4_000_000, 0),
        near=(0, 1),
        mib=16,
    )
    across = exchange(out)
    next_part = call(
        spread_next_kernel,
        square,
        [next_cross],
        [buf(cross), buf(square), sems(2)],
        (200_000_000, 2_000_000, 0),
    )

    first, entering, sent = call(
        middle_kernel,
        (sequence, far(sequence), pair),
        [held_x, across, channel_gain, up, down, queued, next_gain, next_factor],
        [
            buf(x),
            buf(channel_gain),
            buf(up),
            buf(down),
            buf(x),
            buf(norm_gain),
            buf(factor),
            buf(x),
            buf(x),
            buf(shape(2, DEV, 8, HALF)),
            sems(20),
        ],
        (7_000_000_000, 18_000_000, 2_000_000),
        flags,
        near=(1,),
    )
    columns = exchange(sent)
    entered = ahead(entering)
    entered = after(entered, flags)
    columns, entered = lax.optimization_barrier((columns, entered))
    out0, columns1 = call(
        cross_first_kernel,
        (message, far(message)),
        [next_part, columns],
        [buf(square), buf(message), sems(4)],
        (400_000_000, 2_000_000, 0),
        near=(1,),
        mib=12,
    )
    across0 = exchange(out0)
    columns1 = ahead(columns1)
    out1 = call(
        cross_second_kernel,
        message,
        [own_part, columns1],
        [buf(square), buf(message), sems(3)],
        (LONG, 2_000_000, 0),
        near=(1,),
        mib=12,
    )
    across1 = exchange(after(out1, across0, True))
    across0 = ahead(across0)
    bufs = [buf(channel_gain), buf(up), buf(down)]
    other, kept = call(
        last_kernel,
        (far(part_rows), far(part_rows)),
        [entered, across0, channel_gain, up, down],
        [buf(sequence), *bufs, buf(part_rows), buf(part_rows), sems(15)],
        (LONG, 10_000_000, 1_000_000),
        near=(1,),
    )
    second = call(
        final_kernel,
        sequence,
        [hbm(kept), across1, channel_gain, up, down, hbm(other)],
        [buf(part_rows), *bufs, buf(part_rows), buf(sequence), sems(15)],
        (3_000_000_000, 11_000_000, 1_000_000),
        near=(1,),
    )
    return first.reshape(1, *x.shape), second.reshape(1, *x.shape)


def solution(mesh):
    placed = (
        P("section", "seq", None),
        P("seq", None),
        P("section", None),
        P("section", "seq", None, None),
        P("section", "seq", None, None),
        P("section", None),
        P("section", None, None, None),
        P("section", None, None, None),
    )
    return jax.shard_map(
        per_device,
        mesh=mesh,
        in_specs=placed,
        out_specs=(P("section", "seq", None), P("section", "seq", None)),
        check_vma=False,
    )
```

```python
import functools

import jax
import jax.numpy as jnp
from jax import lax
from jax.experimental import pallas as pl
from jax.experimental.pallas import tpu as pltpu
from jax.sharding import PartitionSpec as P

EPS = 1e-05
LONG = 20_000_000_000
D = 1536
HALF = D // 2
BLK = 256
DEV = 64
GROUPS = 4
WIDTH = D // GROUPS
BF = jnp.bfloat16
F32 = jnp.float32


def call(kernel, out_shape, inputs, scratch, cost, flags=None, near=(), mib=32):
    outs = out_shape if isinstance(out_shape, tuple) else (out_shape,)
    held = pl.BlockSpec(memory_space=pl.ANY)
    nearby = pl.BlockSpec(memory_space=pltpu.VMEM)
    scalars = [] if flags is None else [pl.BlockSpec(memory_space=pltpu.SMEM)]
    flops, bytes_accessed, transcendentals = cost
    results = pl.pallas_call(
        kernel,
        out_shape=outs,
        in_specs=scalars + [nearby if n in near else held for n in range(len(inputs))],
        out_specs=[held] * len(outs),
        scratch_shapes=scratch,
        cost_estimate=pl.CostEstimate(
            flops=flops, bytes_accessed=bytes_accessed, transcendentals=transcendentals
        ),
        compiler_params=pltpu.CompilerParams(vmem_limit_bytes=mib * 1024 * 1024),
    )(
        *([] if flags is None else [flags]),
        *[
            pltpu.with_memory_space_constraint(v, pltpu.VMEM) if n in near else v
            for n, v in enumerate(inputs)
        ],
    )
    return results if isinstance(out_shape, tuple) else results[0]


def hbm(value):
    return pltpu.with_memory_space_constraint(value, pltpu.HBM)


class Copies:
    def __init__(self, sems):
        self.sems, self.made = sems, []

    def start(self, source, target):
        copy = pltpu.make_async_copy(source, target, self.sems.at[len(self.made)])
        copy.start()
        self.made.append([copy, False])
        return len(self.made) - 1

    def wait(self, *which):
        for n in which or range(len(self.made)):
            if not self.made[n][1]:
                self.made[n][0].wait()
                self.made[n][1] = True


def columns_of(g):
    return pl.ds(g * WIDTH, WIDTH)


def dot(a, b):
    return jnp.dot(a, b, preferred_element_type=F32)


def onehot(rows, cols, hit):
    r = lax.broadcasted_iota(jnp.int32, (rows, cols), 0)
    c = lax.broadcasted_iota(jnp.int32, (rows, cols), 1)
    return jnp.where(hit(r, c), 1.0, 0.0).astype(BF)


def offsets_of(rows, c):
    return rows.reshape(DEV, 4, -1)[:, 2 * c : 2 * c + 2].reshape(BLK // 2, -1)


def normalize(values, gain):
    scale = lax.rsqrt(jnp.mean(values * values, axis=-1, keepdims=True) + EPS)
    return (values * scale * gain).astype(BF)


def first_kernel(x_ref, gain_ref, factor_ref, out_ref, x_buf, gain_buf, factor_buf, out_buf, sems):
    copies = Copies(sems)
    rows = [pl.ds(b * BLK, BLK) for b in range(2)]
    loads = [
        copies.start(x_ref.at[rows[0]], x_buf.at[rows[0]]),
        copies.start(gain_ref, gain_buf),
        copies.start(factor_ref, factor_buf),
        copies.start(x_ref.at[rows[1]], x_buf.at[rows[1]]),
    ]
    for b in range(2):
        copies.wait(loads[3 * b], loads[1], loads[2])
        normed = normalize(x_buf[rows[b], :].astype(F32), gain_buf[...])
        mixed = dot(factor_buf[b], normed).astype(BF)
        out_buf[:, b] = mixed.reshape(DEV, 4, D)
        copies.start(out_buf.at[:, b], out_ref.at[:, b])
    copies.wait()


def spread(cross, rows, columns, mask):
    n = 2 * BLK
    row = lax.broadcasted_iota(jnp.int32, (n, n), 0)
    col = lax.broadcasted_iota(jnp.int32, (n, n), 1)
    full = dot(dot(onehot(n, n, rows), cross).astype(BF), onehot(128, n, columns))
    return jnp.where(((row ^ col) & mask) == 0, full, 0.0).astype(BF)


def spread_part(cross, c):
    return spread(
        cross,
        lambda r, k: k == (2 * c + (r & 1)) * 128 + (r >> 3) * 2 + ((r >> 1) & 1),
        lambda m, k: m == (k >> 3) * 2 + ((k >> 1) & 1),
        5,
    )


def spread_own_kernel(cross_ref, whole_ref, part_ref, cross_buf, whole_buf, part_buf, sems):
    copies = Copies(sems)
    copies.start(cross_ref, cross_buf)
    copies.wait()
    cross = cross_buf[...].reshape(2 * BLK, 128)
    whole_buf[...] = spread(
        cross,
        lambda r, k: k == (r & 3) * 128 + (r >> 3) * 2 + ((r >> 2) & 1),
        lambda m, k: m == (k >> 3) * 2 + ((k >> 2) & 1),
        3,
    )
    copies.start(whole_buf, whole_ref)
    part_buf[...] = spread_part(cross, 1)
    copies.start(part_buf, part_ref)
    copies.wait()


def spread_next_kernel(cross_ref, part_ref, cross_buf, part_buf, sems):
    copies = Copies(sems)
    copies.start(cross_ref, cross_buf)
    copies.wait()
    part_buf[...] = spread_part(cross_buf[...].reshape(2 * BLK, 128), 0)
    copies.start(part_buf, part_ref)
    copies.wait()


def cross_groups(copies, spread_ref, columns, out_ref, out_buf):
    for g in range(out_ref.shape[-1] // WIDTH):
        part = (slice(None),) * (len(out_ref.shape) - 1) + (columns_of(g),)
        total = dot(spread_ref[...], columns(part).reshape(2 * BLK, WIDTH))
        out_buf[part] = total.astype(BF).reshape(out_ref.shape[:-1] + (WIDTH,))
        copies.start(out_buf.at[part], out_ref.at[part])


def cross_whole_kernel(spread_ref, r_ref, out_ref, out_buf, sems):
    copies = Copies(sems)
    cross_groups(copies, spread_ref, lambda part: r_ref[part], out_ref, out_buf)
    copies.wait()


def cross_first_kernel(spread_ref, r_ref, out_ref, other_ref, spread_buf, out_buf, sems):
    copies = Copies(sems)
    copies.start(spread_ref, spread_buf)
    copies.start(r_ref.at[:, 1], other_ref)
    copies.wait(0)
    cross_groups(copies, spread_buf, lambda part: r_ref[:, 0, :, part[-1]], out_ref, out_buf)
    copies.wait()


def cross_second_kernel(spread_ref, r_ref, out_ref, spread_buf, out_buf, sems):
    copies = Copies(sems)
    copies.start(spread_ref, spread_buf)
    copies.wait()
    cross_groups(copies, spread_buf, lambda part: r_ref[part], out_ref, out_buf)
    copies.wait()


def gelu(hidden):
    value = hidden.astype(BF)
    half = value * BF(0.5)
    inner = value * (BF(0.7978845608028654) + BF(0.7978845608028654 * 0.044715) * (value * value))
    return half + half * jnp.tanh(inner)


def channel_rows(residual, gain, up, down, store):
    normed = normalize(residual, gain)
    for g in range(GROUPS):
        part = slice(g * WIDTH, (g + 1) * WIDTH)
        act = gelu(dot(normed[:, part], up(g)))
        store(g, part, (residual[:, part] + dot(act, down(g))).astype(BF))


def weight_loads(copies, up_ref, down_ref, up_buf, down_buf):
    loads = {}

    def start(g):
        if g < GROUPS and g not in loads:
            loads[g] = (
                copies.start(up_ref.at[g], up_buf.at[g]),
                copies.start(down_ref.at[g], down_buf.at[g]),
            )

    start(0)
    start(1)

    def up(g):
        start(g + 2)
        copies.wait(loads[g][0])
        return up_buf[g]

    def down(g):
        copies.wait(loads[g][1])
        return down_buf[g]

    return up, down, start


def middle_kernel(
    flag_ref,
    x_ref,
    across_ref,
    channel_ref,
    up_ref,
    down_ref,
    queued_ref,
    gain_ref,
    factor_ref,
    first_ref,
    entering_ref,
    out_ref,
    x_buf,
    channel_buf,
    up_buf,
    down_buf,
    queued_buf,
    gain_buf,
    factor_buf,
    first_buf,
    entering_buf,
    out_buf,
    sems,
):
    copies = Copies(sems)
    rows = [pl.ds(b * BLK, BLK) for b in range(2)]
    x_loads = [copies.start(x_ref.at[rows[0]], x_buf.at[rows[0]])]
    channel_load = copies.start(channel_ref, channel_buf)
    up, down, start = weight_loads(copies, up_ref, down_ref, up_buf, down_buf)
    x_loads.append(copies.start(x_ref.at[rows[1]], x_buf.at[rows[1]]))
    for g in range(2, GROUPS):
        start(g)
    late = [
        copies.start(gain_ref, gain_buf),
        copies.start(factor_ref, factor_buf),
        copies.start(queued_ref, queued_buf),
    ]
    last = flag_ref[0] == 1
    copies.wait(channel_load)
    mixed = []
    for b in range(2):

        def store(g, part, value):
            first_buf[rows[b], part] = value

        copies.wait(x_loads[b])
        residual = x_buf[rows[b], :].astype(F32) + across_ref[:, b].reshape(BLK, D).astype(F32)
        channel_rows(residual, channel_buf[...], up, down, store)
        if b == 0:
            copies.wait(*late)
        copies.start(first_buf.at[rows[b]], first_ref.at[rows[b]])
        entering = jnp.where(last, queued_buf[rows[b], :], first_buf[rows[b], :])
        entering_buf[rows[b], :] = entering
        copies.start(entering_buf.at[rows[b]], entering_ref.at[rows[b]])
        mixed.append(dot(factor_buf[b], normalize(entering.astype(F32), gain_buf[...])).astype(BF))
    for c in range(2):
        for b in range(2):
            rows_c = mixed[b].reshape(DEV, 4, D)[:, 2 * c : 2 * c + 2]
            for h in range(2):
                first_row = 4 * h + 2 * b
                half = slice(h * HALF, (h + 1) * HALF)
                out_buf[c, :, first_row : first_row + 2, :] = rows_c[:, :, half]
        copies.start(out_buf.at[c], out_ref.at[:, c])
    copies.wait()


def last_rows(copies, loads, residual_of, across_ref, channel_buf, weights, store):
    up, down, start = weights
    copies.wait(*loads)
    start(2)
    start(3)
    halves = [
        [
            across_ref[:, 4 * h + 2 * b : 4 * h + 2 * b + 2, :].reshape(BLK // 2, HALF)
            for h in range(2)
        ]
        for b in range(2)
    ]
    across = jnp.concatenate([jnp.concatenate(halves[b], axis=1) for b in range(2)], axis=0)
    channel_rows(residual_of() + across.astype(F32), channel_buf[...], up, down, store)


def last_kernel(
    x_ref,
    across_ref,
    channel_ref,
    up_ref,
    down_ref,
    out_ref,
    kept_ref,
    x_buf,
    channel_buf,
    up_buf,
    down_buf,
    out_buf,
    kept_buf,
    sems,
):
    copies = Copies(sems)
    loads = [copies.start(x_ref, x_buf), copies.start(channel_ref, channel_buf)]
    weights = weight_loads(copies, up_ref, down_ref, up_buf, down_buf)

    def rows_of(c):
        picked = [offsets_of(x_buf[b * BLK : (b + 1) * BLK, :], c) for b in range(2)]
        return jnp.concatenate(picked, axis=0)

    def store(g, part, value):
        out_buf[:, part] = value
        copies.start(out_buf.at[:, columns_of(g)], out_ref.at[:, columns_of(g)])

    last_rows(copies, loads, lambda: rows_of(0).astype(F32), across_ref, channel_buf, weights, store)
    kept_buf[...] = rows_of(1)
    copies.start(kept_buf, kept_ref)
    copies.wait()


def final_kernel(
    x_ref,
    across_ref,
    channel_ref,
    up_ref,
    down_ref,
    other_ref,
    out_ref,
    channel_buf,
    up_buf,
    down_buf,
    out_buf,
    sems,
):
    copies = Copies(sems)
    loads = [copies.start(channel_ref, channel_buf)]
    weights = weight_loads(copies, up_ref, down_ref, up_buf, down_buf)

    def store(g, part, value):
        for b in range(2):
            rows = slice(b * (BLK // 2), (b + 1) * (BLK // 2))
            both = [v.reshape(DEV, 2, WIDTH) for v in (other_ref[rows, part], value[rows])]
            joined = jnp.concatenate(both, axis=1).reshape(BLK, WIDTH)
            out_buf[b * BLK : (b + 1) * BLK, part] = joined
        copies.start(out_buf.at[:, columns_of(g)], out_ref.at[:, columns_of(g)])

    last_rows(
        copies, loads, lambda: x_ref[...].astype(F32), across_ref, channel_buf, weights, store
    )
    copies.wait()


def pass_kernel(value_ref, other_ref, out_ref):
    pass


def after(value, other, near=False):
    return pl.pallas_call(
        pass_kernel,
        out_shape=jax.ShapeDtypeStruct(value.shape, value.dtype),
        in_specs=[
            pl.BlockSpec(memory_space=pl.ANY),
            pl.BlockSpec(memory_space=pltpu.VMEM if near else pl.ANY),
        ],
        out_specs=pl.BlockSpec(memory_space=pl.ANY),
        input_output_aliases={0: 0},
        cost_estimate=pl.CostEstimate(flops=LONG, bytes_accessed=0, transcendentals=0),
    )(value, pltpu.with_memory_space_constraint(other, pltpu.VMEM) if near else other)


def shape(*dims):
    return jax.ShapeDtypeStruct(dims, BF)


def exchange(value):
    return lax.all_to_all(hbm(value), "seq", split_axis=0, concat_axis=0, tiled=True)


def per_device(arriving, queued, norm_gain, block_factor, cross_factor, channel_gain, up, down):
    section = lax.axis_index("section")
    count = lax.axis_size("section")
    flags = jnp.full((1,), section == count - 1, jnp.int32)
    x = arriving[0]
    factor, cross, up, down = block_factor[0], cross_factor[0], up[0], down[0]
    held_x, held_factor, held_gain = hbm(x), hbm(factor), hbm(norm_gain)
    cross, up, down, queued, channel_gain = (
        hbm(v) for v in (cross, up, down, queued, channel_gain)
    )

    def ahead(value):
        return lax.ppermute(value, "section", [(s, (s + 1) % count) for s in range(count)])

    def behind(value):
        return lax.ppermute(value, "section", [((s + 1) % count, s) for s in range(count)])

    message, both, pair = shape(DEV, 8, HALF), shape(DEV, 2, 4, D), shape(DEV, 2, 8, HALF)
    square = shape(2 * BLK, 2 * BLK)
    sequence, part_rows = shape(2 * BLK, D), shape(BLK, D)

    def buf(value):
        return pltpu.VMEM(value.shape, value.dtype)

    def far(value):
        return pltpu.HBM(value.shape, value.dtype)

    def sems(n):
        return pltpu.SemaphoreType.DMA((n,))

    sent = call(
        first_kernel,
        both,
        [held_x, held_gain, held_factor],
        [buf(x), buf(norm_gain), buf(factor), buf(both), sems(6)],
        (2_000_000_000, 4_000_000, 0),
    )
    columns = exchange(sent)
    whole, own_part = call(
        spread_own_kernel,
        (square, square),
        [cross],
        [buf(cross), buf(square), buf(square), sems(3)],
        (400_000_000, 3_000_000, 0),
    )
    next_gain, next_factor, next_cross = behind(norm_gain), behind(factor), behind(cross)
    out = call(
        cross_whole_kernel,
        both,
        [whole, columns],
        [buf(both), sems(4)],
        (800_000_000, 4_000_000, 0),
        near=(0, 1),
        mib=16,
    )
    across = exchange(out)
    next_part = call(
        spread_next_kernel,
        square,
        [next_cross],
        [buf(cross), buf(square), sems(2)],
        (200_000_000, 2_000_000, 0),
    )

    first, entering, sent = call(
        middle_kernel,
        (sequence, far(sequence), pair),
        [held_x, across, channel_gain, up, down, queued, next_gain, next_factor],
        [
            buf(x),
            buf(channel_gain),
            buf(up),
            buf(down),
            buf(x),
            buf(norm_gain),
            buf(factor),
            buf(x),
            buf(x),
            buf(shape(2, DEV, 8, HALF)),
            sems(20),
        ],
        (7_000_000_000, 18_000_000, 2_000_000),
        flags,
        near=(1,),
    )
    columns = exchange(sent)
    entered = ahead(entering)
    entered = after(entered, flags)
    columns, entered = lax.optimization_barrier((columns, entered))
    out0, columns1 = call(
        cross_first_kernel,
        (message, far(message)),
        [next_part, columns],
        [buf(square), buf(message), sems(4)],
        (400_000_000, 2_000_000, 0),
        near=(1,),
        mib=12,
    )
    across0 = exchange(out0)
    columns1 = ahead(columns1)
    out1 = call(
        cross_second_kernel,
        message,
        [own_part, columns1],
        [buf(square), buf(message), sems(3)],
        (LONG, 2_000_000, 0),
        near=(1,),
        mib=12,
    )
    across1 = exchange(after(out1, across0, True))
    across0 = ahead(across0)
    bufs = [buf(channel_gain), buf(up), buf(down)]
    other, kept = call(
        last_kernel,
        (part_rows, part_rows),
        [entered, across0, channel_gain, up, down],
        [buf(sequence), *bufs, buf(part_rows), buf(part_rows), sems(15)],
        (LONG, 10_000_000, 1_000_000),
        near=(1,),
    )
    second = call(
        final_kernel,
        sequence,
        [kept, across1, channel_gain, up, down, other],
        [*bufs, buf(sequence), sems(13)],
        (3_000_000_000, 11_000_000, 1_000_000),
        near=(0, 1, 5),
    )
    return first.reshape(1, *x.shape), second.reshape(1, *x.shape)


def solution(mesh):
    placed = (
        P("section", "seq", None),
        P("seq", None),
        P("section", None),
        P("section", "seq", None, None),
        P("section", "seq", None, None),
        P("section", None),
        P("section", None, None, None),
        P("section", None, None, None),
    )
    return jax.shard_map(
        per_device,
        mesh=mesh,
        in_specs=placed,
        out_specs=(P("section", "seq", None), P("section", "seq", None)),
        check_vma=False,
    )
```

```python
import functools

import jax
import jax.numpy as jnp
from jax import lax
from jax.experimental import pallas as pl
from jax.experimental.pallas import tpu as pltpu
from jax.sharding import PartitionSpec as P

EPS = 1e-05
LONG = 20_000_000_000
D = 1536
HALF = D // 2
BLK = 256
DEV = 64
GROUPS = 4
WIDTH = D // GROUPS
BF = jnp.bfloat16
F32 = jnp.float32


def call(kernel, out_shape, inputs, scratch, cost, flags=None, near=(), near_out=(), mib=32):
    outs = out_shape if isinstance(out_shape, tuple) else (out_shape,)
    held = pl.BlockSpec(memory_space=pl.ANY)
    nearby = pl.BlockSpec(memory_space=pltpu.VMEM)
    scalars = [] if flags is None else [pl.BlockSpec(memory_space=pltpu.SMEM)]
    flops, bytes_accessed, transcendentals = cost
    results = pl.pallas_call(
        kernel,
        out_shape=outs,
        in_specs=scalars + [nearby if n in near else held for n in range(len(inputs))],
        out_specs=[nearby if n in near_out else held for n in range(len(outs))],
        scratch_shapes=scratch,
        cost_estimate=pl.CostEstimate(
            flops=flops, bytes_accessed=bytes_accessed, transcendentals=transcendentals
        ),
        compiler_params=pltpu.CompilerParams(vmem_limit_bytes=mib * 1024 * 1024),
    )(
        *([] if flags is None else [flags]),
        *[
            pltpu.with_memory_space_constraint(v, pltpu.VMEM) if n in near else v
            for n, v in enumerate(inputs)
        ],
    )
    return results if isinstance(out_shape, tuple) else results[0]


def hbm(value):
    return pltpu.with_memory_space_constraint(value, pltpu.HBM)


class Copies:
    def __init__(self, sems):
        self.sems, self.made = sems, []

    def start(self, source, target):
        copy = pltpu.make_async_copy(source, target, self.sems.at[len(self.made)])
        copy.start()
        self.made.append([copy, False])
        return len(self.made) - 1

    def wait(self, *which):
        for n in which or range(len(self.made)):
            if not self.made[n][1]:
                self.made[n][0].wait()
                self.made[n][1] = True


def columns_of(g):
    return pl.ds(g * WIDTH, WIDTH)


def dot(a, b):
    return jnp.dot(a, b, preferred_element_type=F32)


def onehot(rows, cols, hit):
    r = lax.broadcasted_iota(jnp.int32, (rows, cols), 0)
    c = lax.broadcasted_iota(jnp.int32, (rows, cols), 1)
    return jnp.where(hit(r, c), 1.0, 0.0).astype(BF)


def offsets_of(rows, c):
    return rows.reshape(DEV, 4, -1)[:, 2 * c : 2 * c + 2].reshape(BLK // 2, -1)


def normalize(values, gain):
    scale = lax.rsqrt(jnp.mean(values * values, axis=-1, keepdims=True) + EPS)
    return (values * scale * gain).astype(BF)


def first_kernel(x_ref, gain_ref, factor_ref, out_ref, x_buf, gain_buf, factor_buf, out_buf, sems):
    copies = Copies(sems)
    rows = [pl.ds(b * BLK, BLK) for b in range(2)]
    loads = [
        copies.start(x_ref.at[rows[0]], x_buf.at[rows[0]]),
        copies.start(gain_ref, gain_buf),
        copies.start(factor_ref, factor_buf),
        copies.start(x_ref.at[rows[1]], x_buf.at[rows[1]]),
    ]
    for b in range(2):
        copies.wait(loads[3 * b], loads[1], loads[2])
        normed = normalize(x_buf[rows[b], :].astype(F32), gain_buf[...])
        mixed = dot(factor_buf[b], normed).astype(BF)
        out_buf[:, b] = mixed.reshape(DEV, 4, D)
        copies.start(out_buf.at[:, b], out_ref.at[:, b])
    copies.wait()


def spread(cross, rows, columns, mask):
    n = 2 * BLK
    row = lax.broadcasted_iota(jnp.int32, (n, n), 0)
    col = lax.broadcasted_iota(jnp.int32, (n, n), 1)
    full = dot(dot(onehot(n, n, rows), cross).astype(BF), onehot(128, n, columns))
    return jnp.where(((row ^ col) & mask) == 0, full, 0.0).astype(BF)


def spread_part(cross, c):
    return spread(
        cross,
        lambda r, k: k == (2 * c + (r & 1)) * 128 + (r >> 3) * 2 + ((r >> 1) & 1),
        lambda m, k: m == (k >> 3) * 2 + ((k >> 1) & 1),
        5,
    )


def spread_own_kernel(cross_ref, whole_ref, cross_buf, whole_buf, sems):
    copies = Copies(sems)
    copies.start(cross_ref, cross_buf)
    copies.wait()
    cross = cross_buf[...].reshape(2 * BLK, 128)
    whole_buf[...] = spread(
        cross,
        lambda r, k: k == (r & 3) * 128 + (r >> 3) * 2 + ((r >> 2) & 1),
        lambda m, k: m == (k >> 3) * 2 + ((k >> 2) & 1),
        3,
    )
    copies.start(whole_buf, whole_ref)
    copies.wait()


def spread_parts_kernel(next_ref, own_ref, part0_ref, part1_ref, cross_buf, part_buf, sems):
    copies = Copies(sems)
    copies.start(next_ref, cross_buf.at[0])
    copies.start(own_ref, cross_buf.at[1])
    copies.wait()
    for c, part_ref in enumerate((part0_ref, part1_ref)):
        part_buf[c] = spread_part(cross_buf[c].reshape(2 * BLK, 128), c)
        copies.start(part_buf.at[c], part_ref)
    copies.wait()


def bring_kernel(x_ref, gain_ref, x_out, gain_out, sems):
    copies = Copies(sems)
    copies.start(x_ref, x_out)
    copies.start(gain_ref, gain_out)
    copies.wait()


def cross_groups(copies, spread_ref, columns, out_ref, out_buf):
    for g in range(out_ref.shape[-1] // WIDTH):
        part = (slice(None),) * (len(out_ref.shape) - 1) + (columns_of(g),)
        total = dot(spread_ref[...], columns(part).reshape(2 * BLK, WIDTH))
        out_buf[part] = total.astype(BF).reshape(out_ref.shape[:-1] + (WIDTH,))
        copies.start(out_buf.at[part], out_ref.at[part])


def cross_whole_kernel(spread_ref, r_ref, out_ref, out_buf, sems):
    copies = Copies(sems)
    cross_groups(copies, spread_ref, lambda part: r_ref[part], out_ref, out_buf)
    copies.wait()


def cross_first_kernel(spread_ref, r_ref, out_ref, other_ref, spread_buf, out_buf, sems):
    copies = Copies(sems)
    copies.start(spread_ref, spread_buf)
    copies.start(r_ref.at[:, 1], other_ref)
    copies.wait(0)
    cross_groups(copies, spread_buf, lambda part: r_ref[:, 0, :, part[-1]], out_ref, out_buf)
    copies.wait()


def cross_second_kernel(spread_ref, r_ref, out_ref, spread_buf, out_buf, sems):
    copies = Copies(sems)
    copies.start(spread_ref, spread_buf)
    copies.wait()
    cross_groups(copies, spread_buf, lambda part: r_ref[part], out_ref, out_buf)
    copies.wait()


def gelu(hidden):
    value = hidden.astype(BF)
    half = value * BF(0.5)
    inner = value * (BF(0.7978845608028654) + BF(0.7978845608028654 * 0.044715) * (value * value))
    return half + half * jnp.tanh(inner)


def channel_rows(residual, gain, up, down, store):
    normed = normalize(residual, gain)
    for g in range(GROUPS):
        part = slice(g * WIDTH, (g + 1) * WIDTH)
        act = gelu(dot(normed[:, part], up(g)))
        store(g, part, (residual[:, part] + dot(act, down(g))).astype(BF))


def weight_loads(copies, up_ref, down_ref, up_buf, down_buf):
    loads = {}

    def start(g):
        if g < GROUPS and g not in loads:
            loads[g] = (
                copies.start(up_ref.at[g], up_buf.at[g]),
                copies.start(down_ref.at[g], down_buf.at[g]),
            )

    start(0)
    start(1)

    def up(g):
        start(g + 2)
        copies.wait(loads[g][0])
        return up_buf[g]

    def down(g):
        copies.wait(loads[g][1])
        return down_buf[g]

    return up, down, start


def middle_kernel(
    flag_ref,
    x_ref,
    across_ref,
    channel_ref,
    up_ref,
    down_ref,
    queued_ref,
    gain_ref,
    factor_ref,
    first_ref,
    entering_ref,
    out_ref,
    up_buf,
    down_buf,
    queued_buf,
    gain_buf,
    factor_buf,
    first_buf,
    entering_buf,
    out_buf,
    sems,
):
    copies = Copies(sems)
    rows = [pl.ds(b * BLK, BLK) for b in range(2)]
    up, down, start = weight_loads(copies, up_ref, down_ref, up_buf, down_buf)
    for g in range(2, GROUPS):
        start(g)
    late = [
        copies.start(gain_ref, gain_buf),
        copies.start(factor_ref, factor_buf),
        copies.start(queued_ref, queued_buf),
    ]
    last = flag_ref[0] == 1
    mixed = []
    for b in range(2):

        def store(g, part, value):
            first_buf[rows[b], part] = value

        residual = x_ref[rows[b], :].astype(F32) + across_ref[:, b].reshape(BLK, D).astype(F32)
        channel_rows(residual, channel_ref[...], up, down, store)
        if b == 0:
            copies.wait(*late)
        copies.start(first_buf.at[rows[b]], first_ref.at[rows[b]])
        entering = jnp.where(last, queued_buf[rows[b], :], first_buf[rows[b], :])
        entering_buf[rows[b], :] = entering
        copies.start(entering_buf.at[rows[b]], entering_ref.at[rows[b]])
        mixed.append(dot(factor_buf[b], normalize(entering.astype(F32), gain_buf[...])).astype(BF))
    for c in range(2):
        for b in range(2):
            rows_c = mixed[b].reshape(DEV, 4, D)[:, 2 * c : 2 * c + 2]
            for h in range(2):
                first_row = 4 * h + 2 * b
                half = slice(h * HALF, (h + 1) * HALF)
                out_buf[c, :, first_row : first_row + 2, :] = rows_c[:, :, half]
        copies.start(out_buf.at[c], out_ref.at[:, c])
    copies.wait()


def last_rows(copies, loads, residual_of, across_ref, channel_buf, weights, store):
    up, down, start = weights
    copies.wait(*loads)
    start(2)
    start(3)
    halves = [
        [
            across_ref[:, 4 * h + 2 * b : 4 * h + 2 * b + 2, :].reshape(BLK // 2, HALF)
            for h in range(2)
        ]
        for b in range(2)
    ]
    across = jnp.concatenate([jnp.concatenate(halves[b], axis=1) for b in range(2)], axis=0)
    channel_rows(residual_of() + across.astype(F32), channel_buf[...], up, down, store)


def last_kernel(
    x_ref,
    across_ref,
    channel_ref,
    up_ref,
    down_ref,
    out_ref,
    kept_ref,
    x_buf,
    channel_buf,
    up_buf,
    down_buf,
    out_buf,
    kept_buf,
    sems,
):
    copies = Copies(sems)
    loads = [copies.start(x_ref, x_buf), copies.start(channel_ref, channel_buf)]
    weights = weight_loads(copies, up_ref, down_ref, up_buf, down_buf)

    def rows_of(c):
        picked = [offsets_of(x_buf[b * BLK : (b + 1) * BLK, :], c) for b in range(2)]
        return jnp.concatenate(picked, axis=0)

    def store(g, part, value):
        out_buf[:, part] = value
        copies.start(out_buf.at[:, columns_of(g)], out_ref.at[:, columns_of(g)])

    last_rows(copies, loads, lambda: rows_of(0).astype(F32), across_ref, channel_buf, weights, store)
    kept_buf[...] = rows_of(1)
    copies.start(kept_buf, kept_ref)
    copies.wait()


def final_kernel(
    x_ref,
    across_ref,
    channel_ref,
    up_ref,
    down_ref,
    other_ref,
    out_ref,
    channel_buf,
    up_buf,
    down_buf,
    out_buf,
    sems,
):
    copies = Copies(sems)
    loads = [copies.start(channel_ref, channel_buf)]
    weights = weight_loads(copies, up_ref, down_ref, up_buf, down_buf)

    def store(g, part, value):
        for b in range(2):
            rows = slice(b * (BLK // 2), (b + 1) * (BLK // 2))
            both = [v.reshape(DEV, 2, WIDTH) for v in (other_ref[rows, part], value[rows])]
            joined = jnp.concatenate(both, axis=1).reshape(BLK, WIDTH)
            out_buf[b * BLK : (b + 1) * BLK, part] = joined
        copies.start(out_buf.at[:, columns_of(g)], out_ref.at[:, columns_of(g)])

    last_rows(
        copies, loads, lambda: x_ref[...].astype(F32), across_ref, channel_buf, weights, store
    )
    copies.wait()


def pass_kernel(value_ref, other_ref, out_ref):
    pass


def after(value, other, near=False):
    return pl.pallas_call(
        pass_kernel,
        out_shape=jax.ShapeDtypeStruct(value.shape, value.dtype),
        in_specs=[
            pl.BlockSpec(memory_space=pl.ANY),
            pl.BlockSpec(memory_space=pltpu.VMEM if near else pl.ANY),
        ],
        out_specs=pl.BlockSpec(memory_space=pl.ANY),
        input_output_aliases={0: 0},
        cost_estimate=pl.CostEstimate(flops=LONG, bytes_accessed=0, transcendentals=0),
    )(value, pltpu.with_memory_space_constraint(other, pltpu.VMEM) if near else other)


def shape(*dims):
    return jax.ShapeDtypeStruct(dims, BF)


def exchange(value):
    return lax.all_to_all(hbm(value), "seq", split_axis=0, concat_axis=0, tiled=True)


def per_device(arriving, queued, norm_gain, block_factor, cross_factor, channel_gain, up, down):
    section = lax.axis_index("section")
    count = lax.axis_size("section")
    flags = jnp.full((1,), section == count - 1, jnp.int32)
    x = arriving[0]
    factor, cross, up, down = block_factor[0], cross_factor[0], up[0], down[0]
    held_x, held_factor, held_gain = hbm(x), hbm(factor), hbm(norm_gain)
    cross, up, down, queued, channel_gain = (
        hbm(v) for v in (cross, up, down, queued, channel_gain)
    )

    def ahead(value):
        return lax.ppermute(value, "section", [(s, (s + 1) % count) for s in range(count)])

    def behind(value):
        return lax.ppermute(value, "section", [((s + 1) % count, s) for s in range(count)])

    message, both, pair = shape(DEV, 8, HALF), shape(DEV, 2, 4, D), shape(DEV, 2, 8, HALF)
    square = shape(2 * BLK, 2 * BLK)
    sequence, part_rows = shape(2 * BLK, D), shape(BLK, D)

    def buf(value):
        return pltpu.VMEM(value.shape, value.dtype)

    def far(value):
        return pltpu.HBM(value.shape, value.dtype)

    def sems(n):
        return pltpu.SemaphoreType.DMA((n,))

    sent = call(
        first_kernel,
        both,
        [held_x, held_gain, held_factor],
        [buf(x), buf(norm_gain), buf(factor), buf(both), sems(6)],
        (2_000_000_000, 4_000_000, 0),
    )
    columns = exchange(sent)
    whole = call(
        spread_own_kernel,
        square,
        [cross],
        [buf(cross), buf(square), sems(2)],
        (200_000_000, 2_000_000, 0),
    )
    next_gain, next_factor, next_cross = behind(norm_gain), behind(factor), behind(cross)
    out = call(
        cross_whole_kernel,
        both,
        [whole, columns],
        [buf(both), sems(4)],
        (800_000_000, 4_000_000, 0),
        near=(0, 1),
        mib=16,
    )
    across = exchange(out)
    near_x, near_gain = call(
        bring_kernel,
        (sequence, jax.ShapeDtypeStruct(channel_gain.shape, F32)),
        [held_x, channel_gain],
        [sems(2)],
        (LONG, 3_000_000, 0),
        near_out=(0, 1),
        mib=2,
    )

    first, entering, sent = call(
        middle_kernel,
        (sequence, far(sequence), pair),
        [near_x, across, near_gain, up, down, queued, next_gain, next_factor],
        [
            buf(up),
            buf(down),
            buf(x),
            buf(norm_gain),
            buf(factor),
            buf(x),
            buf(x),
            buf(shape(2, DEV, 8, HALF)),
            sems(17),
        ],
        (7_000_000_000, 18_000_000, 2_000_000),
        flags,
        near=(0, 1, 2),
    )
    columns = exchange(sent)
    parts = call(
        spread_parts_kernel,
        (square, square),
        [next_cross, cross],
        [buf(shape(2, *cross.shape)), buf(shape(2, 2 * BLK, 2 * BLK)), sems(4)],
        (400_000_000, 2_000_000, 0),
    )
    entered = ahead(entering)
    out0, columns1 = call(
        cross_first_kernel,
        (message, far(message)),
        [parts[0], columns],
        [buf(square), buf(message), sems(4)],
        (400_000_000, 2_000_000, 0),
        near=(1,),
        mib=12,
    )
    across0 = exchange(out0)
    columns1 = ahead(columns1)
    columns1, entered = lax.optimization_barrier((columns1, entered))
    out1 = call(
        cross_second_kernel,
        message,
        [parts[1], columns1],
        [buf(square), buf(message), sems(3)],
        (LONG, 2_000_000, 0),
        near=(1,),
        mib=12,
    )
    across1 = exchange(after(out1, across0, True))
    across0 = ahead(across0)
    bufs = [buf(channel_gain), buf(up), buf(down)]
    other, kept = call(
        last_kernel,
        (part_rows, part_rows),
        [entered, across0, channel_gain, up, down],
        [buf(sequence), *bufs, buf(part_rows), buf(part_rows), sems(15)],
        (LONG, 10_000_000, 1_000_000),
        near=(1,),
    )
    second = call(
        final_kernel,
        sequence,
        [kept, across1, channel_gain, up, down, other],
        [*bufs, buf(sequence), sems(13)],
        (3_000_000_000, 11_000_000, 1_000_000),
        near=(0, 1, 5),
    )
    return first.reshape(1, *x.shape), second.reshape(1, *x.shape)


def solution(mesh):
    placed = (
        P("section", "seq", None),
        P("seq", None),
        P("section", None),
        P("section", "seq", None, None),
        P("section", "seq", None, None),
        P("section", None),
        P("section", None, None, None),
        P("section", None, None, None),
    )
    return jax.shard_map(
        per_device,
        mesh=mesh,
        in_specs=placed,
        out_specs=(P("section", "seq", None), P("section", "seq", None)),
        check_vma=False,
    )
```

```python
import functools

import jax
import jax.numpy as jnp
from jax import lax
from jax.experimental import pallas as pl
from jax.experimental.pallas import tpu as pltpu
from jax.sharding import PartitionSpec as P

EPS = 1e-05
LONG = 20_000_000_000
D = 1536
HALF = D // 2
BLK = 256
DEV = 64
GROUPS = 4
WIDTH = D // GROUPS
BF = jnp.bfloat16
F32 = jnp.float32


def call(kernel, out_shape, inputs, scratch, cost, flags=None, near=(), near_out=(), mib=32):
    outs = out_shape if isinstance(out_shape, tuple) else (out_shape,)
    held = pl.BlockSpec(memory_space=pl.ANY)
    nearby = pl.BlockSpec(memory_space=pltpu.VMEM)
    scalars = [] if flags is None else [pl.BlockSpec(memory_space=pltpu.SMEM)]
    flops, bytes_accessed, transcendentals = cost
    results = pl.pallas_call(
        kernel,
        out_shape=outs,
        in_specs=scalars + [nearby if n in near else held for n in range(len(inputs))],
        out_specs=[nearby if n in near_out else held for n in range(len(outs))],
        scratch_shapes=scratch,
        cost_estimate=pl.CostEstimate(
            flops=flops, bytes_accessed=bytes_accessed, transcendentals=transcendentals
        ),
        compiler_params=pltpu.CompilerParams(vmem_limit_bytes=mib * 1024 * 1024),
    )(
        *([] if flags is None else [flags]),
        *[
            pltpu.with_memory_space_constraint(v, pltpu.VMEM) if n in near else v
            for n, v in enumerate(inputs)
        ],
    )
    return results if isinstance(out_shape, tuple) else results[0]


def hbm(value):
    return pltpu.with_memory_space_constraint(value, pltpu.HBM)


class Copies:
    def __init__(self, sems):
        self.sems, self.made = sems, []

    def start(self, source, target):
        copy = pltpu.make_async_copy(source, target, self.sems.at[len(self.made)])
        copy.start()
        self.made.append([copy, False])
        return len(self.made) - 1

    def wait(self, *which):
        for n in which or range(len(self.made)):
            if not self.made[n][1]:
                self.made[n][0].wait()
                self.made[n][1] = True


def columns_of(g):
    return pl.ds(g * WIDTH, WIDTH)


def dot(a, b):
    return jnp.dot(a, b, preferred_element_type=F32)


def onehot(rows, cols, hit):
    r = lax.broadcasted_iota(jnp.int32, (rows, cols), 0)
    c = lax.broadcasted_iota(jnp.int32, (rows, cols), 1)
    return jnp.where(hit(r, c), 1.0, 0.0).astype(BF)


def part_of(c):
    return slice(c * (BLK // 2), (c + 1) * (BLK // 2))


def normalize(values, gain):
    scale = lax.rsqrt(jnp.mean(values * values, axis=-1, keepdims=True) + EPS)
    return (values * scale * gain).astype(BF)


def first_kernel(x_ref, gain_ref, factor_ref, out_ref, x_buf, gain_buf, factor_buf, out_buf, sems):
    copies = Copies(sems)
    rows = [pl.ds(b * BLK, BLK) for b in range(2)]
    loads = [
        copies.start(x_ref.at[rows[0]], x_buf.at[rows[0]]),
        copies.start(gain_ref, gain_buf),
        copies.start(factor_ref, factor_buf),
        copies.start(x_ref.at[rows[1]], x_buf.at[rows[1]]),
    ]
    for b in range(2):
        copies.wait(loads[3 * b], loads[1], loads[2])
        normed = normalize(x_buf[rows[b], :].astype(F32), gain_buf[...])
        mixed = dot(factor_buf[b], normed).astype(BF)
        for c in range(2):
            out_buf[:, b, 2 * c : 2 * c + 2] = mixed[part_of(c)].reshape(DEV, 2, D)
        copies.start(out_buf.at[:, b], out_ref.at[:, b])
    copies.wait()


def spread(cross, rows, columns, mask):
    n = 2 * BLK
    row = lax.broadcasted_iota(jnp.int32, (n, n), 0)
    col = lax.broadcasted_iota(jnp.int32, (n, n), 1)
    full = dot(dot(onehot(n, n, rows), cross).astype(BF), onehot(128, n, columns))
    return jnp.where(((row ^ col) & mask) == 0, full, 0.0).astype(BF)


def spread_part(cross, c):
    return spread(
        cross,
        lambda r, k: k == (2 * c + (r & 1)) * 128 + (r >> 3) * 2 + ((r >> 1) & 1),
        lambda m, k: m == (k >> 3) * 2 + ((k >> 1) & 1),
        5,
    )


def spread_own_kernel(cross_ref, whole_ref, cross_buf, whole_buf, sems):
    copies = Copies(sems)
    copies.start(cross_ref, cross_buf)
    copies.wait()
    cross = cross_buf[...].reshape(2 * BLK, 128)
    whole_buf[...] = spread(
        cross,
        lambda r, k: k == (r & 3) * 128 + (r >> 3) * 2 + ((r >> 2) & 1),
        lambda m, k: m == (k >> 3) * 2 + ((k >> 2) & 1),
        3,
    )
    copies.start(whole_buf, whole_ref)
    copies.wait()


def spread_parts_kernel(next_ref, own_ref, part0_ref, part1_ref, cross_buf, part_buf, sems):
    copies = Copies(sems)
    copies.start(next_ref, cross_buf.at[0])
    copies.start(own_ref, cross_buf.at[1])
    copies.wait()
    for c, part_ref in enumerate((part0_ref, part1_ref)):
        part_buf[c] = spread_part(cross_buf[c].reshape(2 * BLK, 128), c)
        copies.start(part_buf.at[c], part_ref)
    copies.wait()


def bring_kernel(x_ref, gain_ref, x_out, gain_out, sems):
    copies = Copies(sems)
    copies.start(x_ref, x_out)
    copies.start(gain_ref, gain_out)
    copies.wait()


def cross_groups(copies, spread_ref, columns, out_ref, out_buf):
    for g in range(out_ref.shape[-1] // WIDTH):
        part = (slice(None),) * (len(out_ref.shape) - 1) + (columns_of(g),)
        total = dot(spread_ref[...], columns(part).reshape(2 * BLK, WIDTH))
        out_buf[part] = total.astype(BF).reshape(out_ref.shape[:-1] + (WIDTH,))
        copies.start(out_buf.at[part], out_ref.at[part])


def cross_whole_kernel(spread_ref, r_ref, out_ref, out_buf, sems):
    copies = Copies(sems)
    cross_groups(copies, spread_ref, lambda part: r_ref[part], out_ref, out_buf)
    copies.wait()


def cross_first_kernel(spread_ref, r_ref, out_ref, other_ref, spread_buf, out_buf, sems):
    copies = Copies(sems)
    copies.start(spread_ref, spread_buf)
    copies.start(r_ref.at[:, 1], other_ref)
    copies.wait(0)
    cross_groups(copies, spread_buf, lambda part: r_ref[:, 0, :, part[-1]], out_ref, out_buf)
    copies.wait()


def cross_second_kernel(spread_ref, r_ref, out_ref, spread_buf, out_buf, sems):
    copies = Copies(sems)
    copies.start(spread_ref, spread_buf)
    copies.wait()
    cross_groups(copies, spread_buf, lambda part: r_ref[part], out_ref, out_buf)
    copies.wait()


def gelu(hidden):
    value = hidden.astype(BF)
    half = value * BF(0.5)
    inner = value * (BF(0.7978845608028654) + BF(0.7978845608028654 * 0.044715) * (value * value))
    return half + half * jnp.tanh(inner)


def channel_rows(residual, gain, up, down, store):
    normed = normalize(residual, gain)
    for g in range(GROUPS):
        part = slice(g * WIDTH, (g + 1) * WIDTH)
        act = gelu(dot(normed[:, part], up(g)))
        store(g, part, (residual[:, part] + dot(act, down(g))).astype(BF))


def weight_loads(copies, up_ref, down_ref, up_buf, down_buf):
    loads = {}

    def start(g):
        if g < GROUPS and g not in loads:
            loads[g] = (
                copies.start(up_ref.at[g], up_buf.at[g]),
                copies.start(down_ref.at[g], down_buf.at[g]),
            )

    start(0)
    start(1)

    def up(g):
        start(g + 2)
        copies.wait(loads[g][0])
        return up_buf[g]

    def down(g):
        copies.wait(loads[g][1])
        return down_buf[g]

    return up, down, start


def middle_kernel(
    flag_ref,
    x_ref,
    across_ref,
    channel_ref,
    up_ref,
    down_ref,
    queued_ref,
    gain_ref,
    factor_ref,
    first_ref,
    entering_ref,
    out_ref,
    up_buf,
    down_buf,
    queued_buf,
    gain_buf,
    factor_buf,
    first_buf,
    entering_buf,
    out_buf,
    sems,
):
    copies = Copies(sems)
    rows = [pl.ds(b * BLK, BLK) for b in range(2)]
    up, down, start = weight_loads(copies, up_ref, down_ref, up_buf, down_buf)
    for g in range(2, GROUPS):
        start(g)
    late = [
        copies.start(gain_ref, gain_buf),
        copies.start(factor_ref, factor_buf),
        copies.start(queued_ref, queued_buf),
    ]
    last = flag_ref[0] == 1
    mixed = []
    for b in range(2):

        def store(g, part, value):
            first_buf[rows[b], part] = value

        across = [across_ref[:, b, 2 * c : 2 * c + 2].reshape(BLK // 2, D) for c in range(2)]
        across = jnp.concatenate(across, axis=0).astype(F32)
        residual = x_ref[rows[b], :].astype(F32) + across
        channel_rows(residual, channel_ref[...], up, down, store)
        if b == 0:
            copies.wait(*late)
        copies.start(first_buf.at[rows[b]], first_ref.at[rows[b]])
        entering = jnp.where(last, queued_buf[rows[b], :], first_buf[rows[b], :])
        entering_buf[rows[b], :] = entering
        copies.start(entering_buf.at[rows[b]], entering_ref.at[rows[b]])
        mixed.append(dot(factor_buf[b], normalize(entering.astype(F32), gain_buf[...])).astype(BF))
    for c in range(2):
        for b in range(2):
            rows_c = mixed[b][part_of(c)].reshape(DEV, 2, D)
            for h in range(2):
                first_row = 4 * h + 2 * b
                half = slice(h * HALF, (h + 1) * HALF)
                out_buf[c, :, first_row : first_row + 2, :] = rows_c[:, :, half]
        copies.start(out_buf.at[c], out_ref.at[:, c])
    copies.wait()


def last_rows(copies, loads, residual_of, across_ref, channel_buf, weights, store):
    up, down, start = weights
    copies.wait(*loads)
    start(2)
    start(3)
    halves = [
        [
            across_ref[:, 4 * h + 2 * b : 4 * h + 2 * b + 2, :].reshape(BLK // 2, HALF)
            for h in range(2)
        ]
        for b in range(2)
    ]
    across = jnp.concatenate([jnp.concatenate(halves[b], axis=1) for b in range(2)], axis=0)
    channel_rows(residual_of() + across.astype(F32), channel_buf[...], up, down, store)


def last_kernel(
    x_ref,
    across_ref,
    channel_ref,
    up_ref,
    down_ref,
    out_ref,
    kept_ref,
    x_buf,
    channel_buf,
    up_buf,
    down_buf,
    out_buf,
    kept_buf,
    sems,
):
    copies = Copies(sems)
    loads = [copies.start(x_ref, x_buf), copies.start(channel_ref, channel_buf)]
    weights = weight_loads(copies, up_ref, down_ref, up_buf, down_buf)

    def rows_of(c):
        picked = [x_buf[b * BLK : (b + 1) * BLK, :][part_of(c)] for b in range(2)]
        return jnp.concatenate(picked, axis=0)

    def store(g, part, value):
        out_buf[:, part] = value
        copies.start(out_buf.at[:, columns_of(g)], out_ref.at[:, columns_of(g)])

    last_rows(copies, loads, lambda: rows_of(0).astype(F32), across_ref, channel_buf, weights, store)
    kept_buf[...] = rows_of(1)
    copies.start(kept_buf, kept_ref)
    copies.wait()


def final_kernel(
    x_ref,
    across_ref,
    channel_ref,
    up_ref,
    down_ref,
    other_ref,
    out_ref,
    channel_buf,
    up_buf,
    down_buf,
    out_buf,
    sems,
):
    copies = Copies(sems)
    loads = [copies.start(channel_ref, channel_buf)]
    weights = weight_loads(copies, up_ref, down_ref, up_buf, down_buf)
    rows = BLK // 2

    def store(g, part, value):
        if g == 0:
            for b in range(2):
                target = out_ref.at[pl.ds(b * BLK, rows)]
                copies.start(other_ref.at[pl.ds(b * rows, rows)], target)
        out_buf[:, part] = value
        for b in range(2):
            target = out_ref.at[pl.ds(b * BLK + rows, rows), columns_of(g)]
            copies.start(out_buf.at[pl.ds(b * rows, rows), columns_of(g)], target)

    last_rows(
        copies, loads, lambda: x_ref[...].astype(F32), across_ref, channel_buf, weights, store
    )
    copies.wait()


def pass_kernel(value_ref, other_ref, out_ref):
    pass


def after(value, other, near=False):
    return pl.pallas_call(
        pass_kernel,
        out_shape=jax.ShapeDtypeStruct(value.shape, value.dtype),
        in_specs=[
            pl.BlockSpec(memory_space=pl.ANY),
            pl.BlockSpec(memory_space=pltpu.VMEM if near else pl.ANY),
        ],
        out_specs=pl.BlockSpec(memory_space=pl.ANY),
        input_output_aliases={0: 0},
        cost_estimate=pl.CostEstimate(flops=LONG, bytes_accessed=0, transcendentals=0),
    )(value, pltpu.with_memory_space_constraint(other, pltpu.VMEM) if near else other)


def shape(*dims):
    return jax.ShapeDtypeStruct(dims, BF)


def exchange(value):
    return lax.all_to_all(hbm(value), "seq", split_axis=0, concat_axis=0, tiled=True)


def redistributed(cross):
    device, count = lax.axis_index("seq"), lax.axis_size("seq")
    half = count // 2
    lower = device < half
    first, second = cross[:2], cross[2:]
    to_even = [(s, 2 * s) if s < half else (s, 2 * (s - half) + 1) for s in range(count)]
    to_odd = [(s, 2 * s + 1) if s < half else (s, 2 * (s - half)) for s in range(count)]
    straight = lax.ppermute(jnp.where(lower, first, second), "seq", to_even)
    turned = lax.ppermute(jnp.where(lower, second, first), "seq", to_odd)
    even = device % 2 == 0
    part0 = jnp.where(even, straight, turned)
    part1 = jnp.where(even, turned, straight)
    return jnp.concatenate([part0, part1], axis=0)


def per_device(arriving, queued, norm_gain, block_factor, cross_factor, channel_gain, up, down):
    section = lax.axis_index("section")
    count = lax.axis_size("section")
    flags = jnp.full((1,), section == count - 1, jnp.int32)
    x = arriving[0]
    factor, cross, up, down = block_factor[0], cross_factor[0], up[0], down[0]
    cross = hbm(redistributed(cross))
    held_x, held_factor, held_gain = hbm(x), hbm(factor), hbm(norm_gain)
    up, down, queued, channel_gain = (hbm(v) for v in (up, down, queued, channel_gain))

    def ahead(value):
        return lax.ppermute(value, "section", [(s, (s + 1) % count) for s in range(count)])

    def behind(value):
        return lax.ppermute(value, "section", [((s + 1) % count, s) for s in range(count)])

    message, both, pair = shape(DEV, 8, HALF), shape(DEV, 2, 4, D), shape(DEV, 2, 8, HALF)
    square = shape(2 * BLK, 2 * BLK)
    sequence, part_rows = shape(2 * BLK, D), shape(BLK, D)

    def buf(value):
        return pltpu.VMEM(value.shape, value.dtype)

    def far(value):
        return pltpu.HBM(value.shape, value.dtype)

    def sems(n):
        return pltpu.SemaphoreType.DMA((n,))

    sent = call(
        first_kernel,
        both,
        [held_x, held_gain, held_factor],
        [buf(x), buf(norm_gain), buf(factor), buf(both), sems(6)],
        (2_000_000_000, 4_000_000, 0),
    )
    columns = exchange(sent)
    whole = call(
        spread_own_kernel,
        square,
        [cross],
        [buf(cross), buf(square), sems(2)],
        (200_000_000, 2_000_000, 0),
    )
    next_gain, next_factor, next_cross = behind(norm_gain), behind(factor), behind(cross)
    out = call(
        cross_whole_kernel,
        both,
        [whole, columns],
        [buf(both), sems(4)],
        (800_000_000, 4_000_000, 0),
        near=(0, 1),
        mib=16,
    )
    across = exchange(out)
    near_x, near_gain = call(
        bring_kernel,
        (sequence, jax.ShapeDtypeStruct(channel_gain.shape, F32)),
        [held_x, channel_gain],
        [sems(2)],
        (LONG, 3_000_000, 0),
        near_out=(0, 1),
        mib=2,
    )

    first, entering, sent = call(
        middle_kernel,
        (sequence, far(sequence), pair),
        [near_x, across, near_gain, up, down, queued, next_gain, next_factor],
        [
            buf(up),
            buf(down),
            buf(x),
            buf(norm_gain),
            buf(factor),
            buf(x),
            buf(x),
            buf(shape(2, DEV, 8, HALF)),
            sems(17),
        ],
        (7_000_000_000, 18_000_000, 2_000_000),
        flags,
        near=(0, 1, 2),
    )
    columns = exchange(sent)
    parts = call(
        spread_parts_kernel,
        (square, square),
        [next_cross, cross],
        [buf(shape(2, *cross.shape)), buf(shape(2, 2 * BLK, 2 * BLK)), sems(4)],
        (400_000_000, 2_000_000, 0),
    )
    entered = ahead(entering)
    out0, columns1 = call(
        cross_first_kernel,
        (message, far(message)),
        [parts[0], columns],
        [buf(square), buf(message), sems(4)],
        (400_000_000, 2_000_000, 0),
        near=(1,),
        mib=12,
    )
    across0 = exchange(out0)
    columns1 = ahead(columns1)
    columns1, entered = lax.optimization_barrier((columns1, entered))
    out1 = call(
        cross_second_kernel,
        message,
        [parts[1], columns1],
        [buf(square), buf(message), sems(3)],
        (LONG, 2_000_000, 0),
        near=(1,),
        mib=12,
    )
    across1 = exchange(after(out1, across0, True))
    across0 = ahead(across0)
    bufs = [buf(channel_gain), buf(up), buf(down)]
    other, kept = call(
        last_kernel,
        (part_rows, part_rows),
        [entered, across0, channel_gain, up, down],
        [buf(sequence), *bufs, buf(part_rows), buf(part_rows), sems(15)],
        (LONG, 10_000_000, 1_000_000),
        near=(1,),
    )
    second = call(
        final_kernel,
        sequence,
        [kept, across1, channel_gain, up, down, other],
        [*bufs, buf(part_rows), sems(19)],
        (3_000_000_000, 11_000_000, 1_000_000),
        near=(0, 1, 5),
    )
    return first.reshape(1, *x.shape), second.reshape(1, *x.shape)


def solution(mesh):
    placed = (
        P("section", "seq", None),
        P("seq", None),
        P("section", None),
        P("section", "seq", None, None),
        P("section", "seq", None, None),
        P("section", None),
        P("section", None, None, None),
        P("section", None, None, None),
    )
    return jax.shard_map(
        per_device,
        mesh=mesh,
        in_specs=placed,
        out_specs=(P("section", "seq", None), P("section", "seq", None)),
        check_vma=False,
    )
```

```python
import functools

import jax
import jax.numpy as jnp
from jax import lax
from jax.experimental import pallas as pl
from jax.experimental.pallas import tpu as pltpu
from jax.sharding import PartitionSpec as P

EPS = 1e-05
LONG = 20_000_000_000
D = 1536
HALF = D // 2
BLK = 256
DEV = 64
GROUPS = 4
WIDTH = D // GROUPS
BF = jnp.bfloat16
F32 = jnp.float32


def call(kernel, out_shape, inputs, scratch, cost, flags=None, near=(), near_out=(), mib=32):
    outs = out_shape if isinstance(out_shape, tuple) else (out_shape,)
    held = pl.BlockSpec(memory_space=pl.ANY)
    nearby = pl.BlockSpec(memory_space=pltpu.VMEM)
    scalars = [] if flags is None else [pl.BlockSpec(memory_space=pltpu.SMEM)]
    flops, bytes_accessed, transcendentals = cost
    results = pl.pallas_call(
        kernel,
        out_shape=outs,
        in_specs=scalars + [nearby if n in near else held for n in range(len(inputs))],
        out_specs=[nearby if n in near_out else held for n in range(len(outs))],
        scratch_shapes=scratch,
        cost_estimate=pl.CostEstimate(
            flops=flops, bytes_accessed=bytes_accessed, transcendentals=transcendentals
        ),
        compiler_params=pltpu.CompilerParams(vmem_limit_bytes=mib * 1024 * 1024),
    )(
        *([] if flags is None else [flags]),
        *[
            pltpu.with_memory_space_constraint(v, pltpu.VMEM) if n in near else v
            for n, v in enumerate(inputs)
        ],
    )
    return results if isinstance(out_shape, tuple) else results[0]


def hbm(value):
    return pltpu.with_memory_space_constraint(value, pltpu.HBM)


class Copies:
    def __init__(self, sems):
        self.sems, self.made = sems, []

    def start(self, source, target):
        copy = pltpu.make_async_copy(source, target, self.sems.at[len(self.made)])
        copy.start()
        self.made.append([copy, False])
        return len(self.made) - 1

    def wait(self, *which):
        for n in which or range(len(self.made)):
            if not self.made[n][1]:
                self.made[n][0].wait()
                self.made[n][1] = True


def columns_of(g):
    return pl.ds(g * WIDTH, WIDTH)


def dot(a, b):
    return jnp.dot(a, b, preferred_element_type=F32)


def onehot(rows, cols, hit):
    r = lax.broadcasted_iota(jnp.int32, (rows, cols), 0)
    c = lax.broadcasted_iota(jnp.int32, (rows, cols), 1)
    return jnp.where(hit(r, c), 1.0, 0.0).astype(BF)


def offsets_of(rows, c):
    return rows.reshape(DEV, 4, -1)[:, 2 * c : 2 * c + 2].reshape(BLK // 2, -1)


def normalize(values, gain):
    scale = lax.rsqrt(jnp.mean(values * values, axis=-1, keepdims=True) + EPS)
    return (values * scale * gain).astype(BF)


def first_kernel(x_ref, gain_ref, factor_ref, out_ref, x_buf, gain_buf, factor_buf, out_buf, sems):
    copies = Copies(sems)
    rows = [pl.ds(b * BLK, BLK) for b in range(2)]
    loads = [
        copies.start(x_ref.at[rows[0]], x_buf.at[rows[0]]),
        copies.start(gain_ref, gain_buf),
        copies.start(factor_ref, factor_buf),
        copies.start(x_ref.at[rows[1]], x_buf.at[rows[1]]),
    ]
    for b in range(2):
        copies.wait(loads[3 * b], loads[1], loads[2])
        normed = normalize(x_buf[rows[b], :].astype(F32), gain_buf[...])
        mixed = dot(factor_buf[b], normed).astype(BF)
        out_buf[:, b] = mixed.reshape(DEV, 4, D)
        copies.start(out_buf.at[:, b], out_ref.at[:, b])
    copies.wait()


def spread(cross, rows, columns, mask):
    n = 2 * BLK
    row = lax.broadcasted_iota(jnp.int32, (n, n), 0)
    col = lax.broadcasted_iota(jnp.int32, (n, n), 1)
    full = dot(dot(onehot(n, n, rows), cross).astype(BF), onehot(128, n, columns))
    return jnp.where(((row ^ col) & mask) == 0, full, 0.0).astype(BF)


def spread_part(cross, c):
    return spread(
        cross,
        lambda r, k: k == (2 * c + (r & 1)) * 128 + (r >> 3) * 2 + ((r >> 1) & 1),
        lambda m, k: m == (k >> 3) * 2 + ((k >> 1) & 1),
        5,
    )


def spread_own_kernel(cross_ref, whole_ref, cross_buf, whole_buf, sems):
    copies = Copies(sems)
    copies.start(cross_ref, cross_buf)
    copies.wait()
    cross = cross_buf[...].reshape(2 * BLK, 128)
    whole_buf[...] = spread(
        cross,
        lambda r, k: k == (r & 3) * 128 + (r >> 3) * 2 + ((r >> 2) & 1),
        lambda m, k: m == (k >> 3) * 2 + ((k >> 2) & 1),
        3,
    )
    copies.start(whole_buf, whole_ref)
    copies.wait()


def spread_parts_kernel(next_ref, own_ref, part0_ref, part1_ref, cross_buf, part_buf, sems):
    copies = Copies(sems)
    copies.start(next_ref, cross_buf.at[0])
    copies.start(own_ref, cross_buf.at[1])
    copies.wait()
    for c, part_ref in enumerate((part0_ref, part1_ref)):
        part_buf[c] = spread_part(cross_buf[c].reshape(2 * BLK, 128), c)
        copies.start(part_buf.at[c], part_ref)
    copies.wait()


def bring_kernel(x_ref, gain_ref, x_out, gain_out, sems):
    copies = Copies(sems)
    copies.start(x_ref, x_out)
    copies.start(gain_ref, gain_out)
    copies.wait()


def cross_groups(copies, spread_ref, columns, out_ref, out_buf):
    for g in range(out_ref.shape[-1] // WIDTH):
        part = (slice(None),) * (len(out_ref.shape) - 1) + (columns_of(g),)
        total = dot(spread_ref[...], columns(part).reshape(2 * BLK, WIDTH))
        out_buf[part] = total.astype(BF).reshape(out_ref.shape[:-1] + (WIDTH,))
        copies.start(out_buf.at[part], out_ref.at[part])


def cross_whole_kernel(spread_ref, r_ref, out_ref, out_buf, sems):
    copies = Copies(sems)
    cross_groups(copies, spread_ref, lambda part: r_ref[part], out_ref, out_buf)
    copies.wait()


def cross_first_kernel(spread_ref, r_ref, out_ref, other_ref, spread_buf, out_buf, sems):
    copies = Copies(sems)
    copies.start(spread_ref, spread_buf)
    copies.start(r_ref.at[:, 1], other_ref)
    copies.wait(0)
    cross_groups(copies, spread_buf, lambda part: r_ref[:, 0, :, part[-1]], out_ref, out_buf)
    copies.wait()


def cross_second_kernel(spread_ref, r_ref, out_ref, spread_buf, out_buf, sems):
    copies = Copies(sems)
    copies.start(spread_ref, spread_buf)
    copies.wait()
    cross_groups(copies, spread_buf, lambda part: r_ref[part], out_ref, out_buf)
    copies.wait()


def gelu(hidden):
    value = hidden.astype(BF)
    half = value * BF(0.5)
    inner = value * (BF(0.7978845608028654) + BF(0.7978845608028654 * 0.044715) * (value * value))
    return half + half * jnp.tanh(inner)


def channel_rows(residual, gain, up, down, store):
    normed = normalize(residual, gain)
    for g in range(GROUPS):
        part = slice(g * WIDTH, (g + 1) * WIDTH)
        act = gelu(dot(normed[:, part], up(g)))
        store(g, part, (residual[:, part] + dot(act, down(g))).astype(BF))


def weight_loads(copies, up_ref, down_ref, up_buf, down_buf):
    loads = {}

    def start(g):
        if g < GROUPS and g not in loads:
            loads[g] = (
                copies.start(up_ref.at[g], up_buf.at[g]),
                copies.start(down_ref.at[g], down_buf.at[g]),
            )

    start(0)
    start(1)

    def up(g):
        start(g + 2)
        copies.wait(loads[g][0])
        return up_buf[g]

    def down(g):
        copies.wait(loads[g][1])
        return down_buf[g]

    return up, down


def middle_kernel(
    flag_ref,
    x_ref,
    across_ref,
    channel_ref,
    up_ref,
    down_ref,
    queued_ref,
    gain_ref,
    factor_ref,
    first_ref,
    entering_ref,
    out_ref,
    up_buf,
    down_buf,
    queued_buf,
    gain_buf,
    factor_buf,
    first_buf,
    entering_buf,
    out_buf,
    sems,
):
    copies = Copies(sems)
    rows = [pl.ds(b * BLK, BLK) for b in range(2)]
    up, down = weight_loads(copies, up_ref, down_ref, up_buf, down_buf)
    late = []
    last = flag_ref[0] == 1
    mixed = []
    for b in range(2):

        def store(g, part, value):
            first_buf[rows[b], part] = value
            if b == 0 and g == 1:
                late.append(copies.start(gain_ref, gain_buf))
                late.append(copies.start(factor_ref, factor_buf))
                late.append(copies.start(queued_ref, queued_buf))

        residual = x_ref[rows[b], :].astype(F32) + across_ref[:, b].reshape(BLK, D).astype(F32)
        channel_rows(residual, channel_ref[...], up, down, store)
        if b == 0:
            copies.wait(*late)
        copies.start(first_buf.at[rows[b]], first_ref.at[rows[b]])
        entering = jnp.where(last, queued_buf[rows[b], :], first_buf[rows[b], :])
        entering_buf[rows[b], :] = entering
        copies.start(entering_buf.at[rows[b]], entering_ref.at[rows[b]])
        mixed.append(dot(factor_buf[b], normalize(entering.astype(F32), gain_buf[...])).astype(BF))
    for c in range(2):
        for b in range(2):
            rows_c = mixed[b].reshape(DEV, 4, D)[:, 2 * c : 2 * c + 2]
            for h in range(2):
                first_row = 4 * h + 2 * b
                half = slice(h * HALF, (h + 1) * HALF)
                out_buf[c, :, first_row : first_row + 2, :] = rows_c[:, :, half]
        copies.start(out_buf.at[c], out_ref.at[:, c])
    copies.wait()


def last_rows(copies, loads, residual_of, across_ref, channel_buf, weights, store):
    up, down = weights
    copies.wait(*loads)
    halves = [
        [
            across_ref[:, 4 * h + 2 * b : 4 * h + 2 * b + 2, :].reshape(BLK // 2, HALF)
            for h in range(2)
        ]
        for b in range(2)
    ]
    across = jnp.concatenate([jnp.concatenate(halves[b], axis=1) for b in range(2)], axis=0)
    channel_rows(residual_of() + across.astype(F32), channel_buf[...], up, down, store)


def last_kernel(
    x_ref,
    across_ref,
    channel_ref,
    up_ref,
    down_ref,
    out_ref,
    kept_ref,
    x_buf,
    channel_buf,
    up_buf,
    down_buf,
    out_buf,
    kept_buf,
    sems,
):
    copies = Copies(sems)
    loads = [copies.start(x_ref, x_buf), copies.start(channel_ref, channel_buf)]
    weights = weight_loads(copies, up_ref, down_ref, up_buf, down_buf)

    def rows_of(c):
        picked = [offsets_of(x_buf[b * BLK : (b + 1) * BLK, :], c) for b in range(2)]
        return jnp.concatenate(picked, axis=0)

    def store(g, part, value):
        out_buf[:, part] = value
        copies.start(out_buf.at[:, columns_of(g)], out_ref.at[:, columns_of(g)])

    last_rows(copies, loads, lambda: rows_of(0).astype(F32), across_ref, channel_buf, weights, store)
    kept_buf[...] = rows_of(1)
    copies.start(kept_buf, kept_ref)
    copies.wait()


def final_kernel(
    x_ref,
    across_ref,
    channel_ref,
    up_ref,
    down_ref,
    other_ref,
    out_ref,
    channel_buf,
    up_buf,
    down_buf,
    out_buf,
    sems,
):
    copies = Copies(sems)
    loads = [copies.start(channel_ref, channel_buf)]
    weights = weight_loads(copies, up_ref, down_ref, up_buf, down_buf)

    def put(c, rows, part):
        for b in range(2):
            pairs = rows[b * (BLK // 2) : (b + 1) * (BLK // 2)].reshape(DEV // 2, 4, -1)
            for d in range(2):
                row = 4 * d + 2 * c
                out_buf[b, :, row : row + 2, part] = pairs[:, 2 * d : 2 * d + 2]

    def store(g, part, value):
        put(0, other_ref[:, part], part)
        put(1, value, part)
        columns = columns_of(g)
        copies.start(out_buf.at[:, :, :, columns], out_ref.at[:, :, :, columns])

    last_rows(
        copies, loads, lambda: x_ref[...].astype(F32), across_ref, channel_buf, weights, store
    )
    copies.wait()


def pass_kernel(value_ref, other_ref, out_ref):
    pass


def after(value, other, near=False):
    return pl.pallas_call(
        pass_kernel,
        out_shape=jax.ShapeDtypeStruct(value.shape, value.dtype),
        in_specs=[
            pl.BlockSpec(memory_space=pl.ANY),
            pl.BlockSpec(memory_space=pltpu.VMEM if near else pl.ANY),
        ],
        out_specs=pl.BlockSpec(memory_space=pl.ANY),
        input_output_aliases={0: 0},
        cost_estimate=pl.CostEstimate(flops=LONG, bytes_accessed=0, transcendentals=0),
    )(value, pltpu.with_memory_space_constraint(other, pltpu.VMEM) if near else other)


def shape(*dims):
    return jax.ShapeDtypeStruct(dims, BF)


def exchange(value):
    return lax.all_to_all(hbm(value), "seq", split_axis=0, concat_axis=0, tiled=True)


def per_device(arriving, queued, norm_gain, block_factor, cross_factor, channel_gain, up, down):
    section = lax.axis_index("section")
    count = lax.axis_size("section")
    flags = jnp.full((1,), section == count - 1, jnp.int32)
    x = arriving[0]
    factor, cross, up, down = block_factor[0], cross_factor[0], up[0], down[0]
    held_x, held_factor, held_gain = hbm(x), hbm(factor), hbm(norm_gain)
    cross, up, down, queued, channel_gain = (
        hbm(v) for v in (cross, up, down, queued, channel_gain)
    )

    def ahead(value):
        return lax.ppermute(value, "section", [(s, (s + 1) % count) for s in range(count)])

    def behind(value):
        return lax.ppermute(value, "section", [((s + 1) % count, s) for s in range(count)])

    message, both, pair = shape(DEV, 8, HALF), shape(DEV, 2, 4, D), shape(DEV, 2, 8, HALF)
    square = shape(2 * BLK, 2 * BLK)
    sequence, part_rows = shape(2 * BLK, D), shape(BLK, D)

    def buf(value):
        return pltpu.VMEM(value.shape, value.dtype)

    def far(value):
        return pltpu.HBM(value.shape, value.dtype)

    def sems(n):
        return pltpu.SemaphoreType.DMA((n,))

    sent = call(
        first_kernel,
        both,
        [held_x, held_gain, held_factor],
        [buf(x), buf(norm_gain), buf(factor), buf(both), sems(6)],
        (2_000_000_000, 4_000_000, 0),
    )
    columns = exchange(sent)
    whole = call(
        spread_own_kernel,
        square,
        [cross],
        [buf(cross), buf(square), sems(2)],
        (200_000_000, 2_000_000, 0),
    )
    next_gain, next_factor, next_cross = behind(norm_gain), behind(factor), behind(cross)
    out = call(
        cross_whole_kernel,
        both,
        [whole, columns],
        [buf(both), sems(4)],
        (800_000_000, 4_000_000, 0),
        near=(0, 1),
        mib=16,
    )
    across = exchange(out)
    near_x, near_gain = call(
        bring_kernel,
        (sequence, jax.ShapeDtypeStruct(channel_gain.shape, F32)),
        [held_x, channel_gain],
        [sems(2)],
        (LONG, 3_000_000, 0),
        near_out=(0, 1),
        mib=2,
    )

    first, entering, sent = call(
        middle_kernel,
        (sequence, far(sequence), pair),
        [near_x, across, near_gain, up, down, queued, next_gain, next_factor],
        [
            buf(up),
            buf(down),
            buf(x),
            buf(norm_gain),
            buf(factor),
            buf(x),
            buf(x),
            buf(shape(2, DEV, 8, HALF)),
            sems(17),
        ],
        (7_000_000_000, 18_000_000, 2_000_000),
        flags,
        near=(0, 1, 2),
    )
    columns = exchange(sent)
    parts = call(
        spread_parts_kernel,
        (square, square),
        [next_cross, cross],
        [buf(shape(2, *cross.shape)), buf(shape(2, 2 * BLK, 2 * BLK)), sems(4)],
        (400_000_000, 2_000_000, 0),
    )
    entered = ahead(entering)
    out0, columns1 = call(
        cross_first_kernel,
        (message, far(message)),
        [parts[0], columns],
        [buf(square), buf(message), sems(4)],
        (400_000_000, 2_000_000, 0),
        near=(1,),
        mib=12,
    )
    across0 = exchange(out0)
    columns1 = ahead(columns1)
    columns1, entered = lax.optimization_barrier((columns1, entered))
    out1 = call(
        cross_second_kernel,
        message,
        [parts[1], columns1],
        [buf(square), buf(message), sems(3)],
        (LONG, 2_000_000, 0),
        near=(1,),
        mib=12,
    )
    across1 = exchange(after(out1, across0, True))
    across0 = ahead(across0)
    bufs = [buf(channel_gain), buf(up), buf(down)]
    other, kept = call(
        last_kernel,
        (part_rows, part_rows),
        [entered, across0, channel_gain, up, down],
        [buf(sequence), *bufs, buf(part_rows), buf(part_rows), sems(15)],
        (LONG, 10_000_000, 1_000_000),
        near=(1,),
    )
    paired = shape(2, DEV // 2, 8, D)
    second = call(
        final_kernel,
        paired,
        [kept, across1, channel_gain, up, down, other],
        [*bufs, buf(paired), sems(13)],
        (3_000_000_000, 11_000_000, 1_000_000),
        near=(0, 1, 5),
    )
    return first.reshape(1, *x.shape), second.reshape(1, *x.shape)


def solution(mesh):
    placed = (
        P("section", "seq", None),
        P("seq", None),
        P("section", None),
        P("section", "seq", None, None),
        P("section", "seq", None, None),
        P("section", None),
        P("section", None, None, None),
        P("section", None, None, None),
    )
    return jax.shard_map(
        per_device,
        mesh=mesh,
        in_specs=placed,
        out_specs=(P("section", "seq", None), P("section", "seq", None)),
        check_vma=False,
    )
```
